32 devices in a mesh: seq: 8 (over z, y), tensor: 4 (over x, core).
Axes of the slice: x: 2, y: 2, z: 4, core: 2. Of those that a mesh axis runs over, the one named last changes fastest.
Arguments:
- tokens: bfloat16 [128, 4, 3072], P('seq'), may hold values from -6 to 6
- lengths: int32 [128], replicated, may hold values from 1 to 16384, as said below
- page_request: int32 [1024], P('seq'), may hold values from 0 to 127, as said below
- page_block: int32 [1024], P('seq'), may hold values from 0 to 128, as said below
- k_cache: bfloat16 [1024, 8, 128, 128], P('seq', 'tensor'), may hold values from -330 to 330
- v_cache: bfloat16 [1024, 8, 128, 128], P('seq', 'tensor'), may hold values from -6 to 6
- attn_gain: bfloat16 [3072], replicated, may hold values from 0.099609375 to 1.8984375
- w_query: bfloat16 [3072, 3072], P(None, 'tensor'), may hold values from -0.109375 to 0.109375
- w_key: bfloat16 [3072, 1024], P(None, 'tensor'), may hold values from -0.109375 to 0.109375
- w_value: bfloat16 [3072, 1024], P(None, 'tensor'), may hold values from -0.109375 to 0.109375
- w_out: bfloat16 [3072, 3072], P('tensor'), may hold values from -0.109375 to 0.109375
- mlp_gain: bfloat16 [3072], replicated, may hold values from 0.099609375 to 1.8984375
- w_gate: bfloat16 [3072, 4096], P(None, 'tensor'), may hold values from -0.109375 to 0.109375
- w_up: bfloat16 [3072, 4096], P(None, 'tensor'), may hold values from -0.109375 to 0.109375
- w_down: bfloat16 [4096, 3072], P('tensor'), may hold values from -0.09375 to 0.09375
Outputs:
- layer_out: bfloat16 [128, 4, 3072], P('seq', None, 'tensor')
The draws below stay inside these ranges and needn't reach their ends.
Inputs may be any that keep to these rules, and one draw needn't show every extreme that they name: `lengths`: A request r whose index is a multiple of 32 has a long cache, within 128 tokens of 16384; the others have at most 511. Request 0 has exactly 16384. `page_request`: each pair of a long request and a page number below 128, or of a short request and a page number below 4, appears in exactly one slot; slots of pages at or beyond a request's length hold no used position. A short request's pages lie in the slots of the seq index that holds its tokens. `page_block`: slots of page number 128 hold no used position.
All inputs are finite; a program needn't handle non-finite values.
Results may differ from the reference program's by a relative error of at most 0.012.
Values may be sent and summed in bfloat16 or wider, within the bound.
A program may use at most 128 MiB of HBM per device.

```python
import math
import jax
import jax.numpy as jnp
from jax import lax

D = 3072
HQ = 24
KVH = 8
HD = 128
FF = 4096
NEW = 4
PAGE = 128
LONG_MAX = 16384
SHORT_MAX = 511
REQ_DEV = 16
G = 3
REQS = 128
LONGS = 4
LONG_BLK = 128
SHORT_BLK = 4
PAGES_DEV = 128
POOL = 1024


def shuffle_row(row_key):
    return jax.random.permutation(row_key, PAGES_DEV)


def page_layout(key):
    base_key = jax.random.fold_in(key, 11)
    key_long, key_short, key_rotation, key_shuffle = jax.random.split(base_key, 4)
    seq_count = REQS // REQ_DEV
    requests = jnp.arange(REQS, dtype=jnp.int32)
    is_long = requests % (2 * REQ_DEV) == 0
    long_length = LONG_MAX - jax.random.randint(key_long, (REQS,), 0, PAGE, dtype=jnp.int32)
    short_length = jax.random.randint(key_short, (REQS,), 1, SHORT_MAX + 1, dtype=jnp.int32)
    lengths = jnp.where(is_long, long_length, short_length)
    lengths = jnp.where(requests == 0, LONG_MAX, lengths)
    lengths = jnp.where(requests == 1, SHORT_MAX, lengths)
    lengths = jnp.where(requests == 2, 1, lengths).astype(jnp.int32)
    per_long = LONG_BLK // seq_count
    rotation = jax.random.randint(key_rotation, (LONGS,), 0, seq_count, dtype=jnp.int32)
    device_column = jnp.arange(seq_count, dtype=jnp.int32)[:, None]
    long_slot = jnp.arange(LONGS * per_long, dtype=jnp.int32)[None, :]
    long_index = long_slot // per_long
    long_request = jnp.broadcast_to(long_index * 2 * REQ_DEV, (seq_count, LONGS * per_long))
    long_block = long_slot % per_long * seq_count + (device_column - rotation[long_index]) % seq_count
    short_slot = jnp.arange(REQ_DEV * SHORT_BLK, dtype=jnp.int32)[None, :]
    short_request = device_column * REQ_DEV + short_slot // SHORT_BLK
    short_block = jnp.where(short_request % (2 * REQ_DEV) == 0, LONG_BLK, short_slot % SHORT_BLK)
    owners = jnp.concatenate([long_request, short_request], axis=1)
    blocks = jnp.concatenate([long_block, short_block], axis=1)
    shuffle = jax.vmap(shuffle_row)(jax.random.split(key_shuffle, seq_count))
    owners = jnp.take_along_axis(owners, shuffle, axis=1).reshape(POOL).astype(jnp.int32)
    blocks = jnp.take_along_axis(blocks, shuffle, axis=1).reshape(POOL).astype(jnp.int32)
    return (lengths, owners, blocks)


def draw_lengths(key, part):
    return page_layout(key)[0]


def draw_page_request(key, part):
    return page_layout(key)[1]


def draw_page_block(key, part):
    return page_layout(key)[2]


def draw_k_cache(key, part):
    base_key = jax.random.fold_in(key, 23)
    key_base = jax.random.fold_in(base_key, 0)
    shape = (POOL, KVH, PAGE, HD)
    return jnp.clip(2.5 * jax.random.normal(key_base, shape, jnp.float32), -16.0, 16.0).astype(jnp.bfloat16)


def level_of(rng, dims, shards, least, largest):
    gain = 1.0
    for dim, blocks in shards:
        heights = jax.random.uniform(jax.random.fold_in(jax.random.fold_in(rng, 6), dim), (blocks,), jnp.float32, least / len(shards), largest / len(shards))
        gain = gain * jnp.repeat(jnp.exp(heights), dims[dim] // blocks).reshape((-1,) + (1,) * (len(dims) - 1 - dim))
    return gain


def normal_values(own_key, dims, deviation, limit, shards=(), kind=jnp.bfloat16):
    gain = level_of(own_key, dims, shards, -0.22, 0.18) if shards else 1.0
    array = jax.random.normal(own_key, dims, jnp.float32) * deviation * gain
    return jnp.minimum(jnp.maximum(array, -limit), limit).astype(kind)


def setup_inputs(seed: int = 0) -> dict:
    streams_of = jax.random.split(jax.random.key(seed), 16)
    return {
        "tokens": normal_values(streams_of[0], (REQS, NEW, D), 1.0, 6.0, ((0, 8),)),
        "lengths": draw_lengths(jax.random.fold_in(streams_of[15], 71), 0),
        "page_request": draw_page_request(jax.random.fold_in(streams_of[15], 71), 0),
        "page_block": draw_page_block(jax.random.fold_in(streams_of[15], 71), 0),
        "k_cache": draw_k_cache(jax.random.fold_in(streams_of[15], 71), 0),
        "v_cache": normal_values(streams_of[5], (POOL, KVH, PAGE, HD), 1.0, 6.0, ((0, 8), (1, 4))),
        "attn_gain": jnp.clip(1.0 + 0.18 * jax.random.normal(streams_of[6], (D,), jnp.float32), 0.099609375, 1.8984375).astype(jnp.bfloat16),
        "w_query": normal_values(streams_of[7], (D, HQ * HD), D ** -0.5, 0.109375, ((1, 4),)),
        "w_key": normal_values(streams_of[8], (D, KVH * HD), D ** -0.5, 0.109375, ((1, 4),)),
        "w_value": normal_values(streams_of[9], (D, KVH * HD), D ** -0.5, 0.109375, ((1, 4),)),
        "w_out": normal_values(streams_of[10], (HQ * HD, D), (HQ * HD) ** -0.5, 0.109375, ((0, 4),)),
        "mlp_gain": jnp.clip(1.0 + 0.18 * jax.random.normal(streams_of[11], (D,), jnp.float32), 0.099609375, 1.8984375).astype(jnp.bfloat16),
        "w_gate": normal_values(streams_of[12], (D, FF), D ** -0.5, 0.109375, ((1, 4),)),
        "w_up": normal_values(streams_of[13], (D, FF), D ** -0.5, 0.109375, ((1, 4),)),
        "w_down": normal_values(streams_of[14], (FF, D), FF ** -0.5, 0.09375, ((0, 4),)),
    }


EPSILON = 1e-05
NEGATIVE = -1e+30
ROPE_BASE = 500000.0

def rms_norm(values, gains):
    mean_square = lax.optimization_barrier(jnp.mean(values * values, axis=-1, keepdims=True))
    return values * lax.rsqrt(mean_square + EPSILON) * gains.astype(jnp.float32)

def rotary(values, position):
    head_width = values.shape[-1]
    half_width = head_width // 2
    inverse = 1.0 / ROPE_BASE ** (jnp.arange(half_width, dtype=jnp.float32) * 2.0 / head_width)
    angle = position.astype(jnp.float32)[..., None, None] * inverse
    cosine = jnp.cos(angle)
    sine_table = jnp.sin(angle)
    front_half = values[..., :half_width]
    back_half = values[..., half_width:]
    return jnp.concatenate([front_half * cosine - back_half * sine_table, back_half * cosine + front_half * sine_table], axis=-1)

def reference(tokens, lengths, page_request, page_block, k_cache, v_cache, attn_gain, w_query, w_key, w_value, w_out, mlp_gain, w_gate, w_up, w_down):
    row_count = REQS * NEW
    lanes = NEW * G
    score_scale = 1.0 / math.sqrt(HD)
    values_in = tokens.astype(jnp.float32)
    normed_in = rms_norm(values_in, attn_gain).astype(jnp.bfloat16).reshape(row_count, D)
    position = lengths[:, None] + jnp.arange(NEW, dtype=jnp.int32)[None, :]
    queries = jnp.dot(normed_in, w_query, preferred_element_type=jnp.float32).reshape(REQS, NEW, HQ, HD)
    queries = rotary(queries, position).astype(jnp.bfloat16)
    key_new = jnp.dot(normed_in, w_key, preferred_element_type=jnp.float32).reshape(REQS, NEW, KVH, HD)
    key_new = rotary(key_new, position).astype(jnp.bfloat16)
    value_new = jnp.dot(normed_in, w_value, preferred_element_type=jnp.float32).astype(jnp.bfloat16).reshape(REQS, NEW, KVH, HD)
    offsets = jnp.arange(PAGE, dtype=jnp.int32)
    owner_length = lengths[page_request]
    is_valid = page_block[:, None] * PAGE + offsets[None, :] < owner_length[:, None]
    causal = (jnp.arange(lanes, dtype=jnp.int32) // G)[:, None] >= jnp.arange(NEW, dtype=jnp.int32)[None, :]

    def one_head(operands):
        head_query, head_keys, head_values, fresh_key, fresh_value = operands
        flat_query = head_query.reshape(REQS, lanes, HD)
        chosen = flat_query[page_request].astype(jnp.float32)
        scores = jnp.einsum('pqd,pkd->pqk', chosen, head_keys.astype(jnp.float32)) * score_scale
        scores = jnp.where(is_valid[:, None, :], scores, NEGATIVE)
        page_max = lax.optimization_barrier(jnp.max(scores, axis=-1))
        cache_max = jnp.full((REQS, lanes), NEGATIVE, jnp.float32).at[page_request].max(page_max)
        fresh_scores = jnp.einsum('rqd,rsd->rqs', flat_query.astype(jnp.float32), fresh_key.astype(jnp.float32)) * score_scale
        fresh_scores = jnp.where(causal[None], fresh_scores, NEGATIVE)
        row_max = jnp.maximum(cache_max, lax.optimization_barrier(jnp.max(fresh_scores, axis=-1)))
        weights = jnp.where(is_valid[:, None, :], jnp.exp(scores - row_max[page_request][:, :, None]), 0.0).astype(jnp.bfloat16)
        fresh_weights = jnp.where(causal[None], jnp.exp(fresh_scores - row_max[:, :, None]), 0.0).astype(jnp.bfloat16)
        weight_total = jnp.zeros((REQS, lanes), jnp.float32).at[page_request].add(lax.optimization_barrier(jnp.sum(weights.astype(jnp.float32), axis=-1)))
        weight_total = weight_total + lax.optimization_barrier(jnp.sum(fresh_weights.astype(jnp.float32), axis=-1))
        page_sum = jnp.einsum('pqk,pkd->pqd', weights.astype(jnp.float32), head_values.astype(jnp.float32))
        summed = jnp.zeros((REQS, lanes, HD), jnp.float32).at[page_request].add(page_sum)
        summed = summed + jnp.einsum('rqs,rsd->rqd', fresh_weights.astype(jnp.float32), fresh_value.astype(jnp.float32))
        return (summed / weight_total[:, :, None]).astype(jnp.bfloat16)
    head_queries = jnp.moveaxis(queries.reshape(REQS, NEW, KVH, G, HD), 2, 0)
    head_keys = jnp.moveaxis(k_cache, 1, 0)
    head_values = jnp.moveaxis(v_cache, 1, 0)
    fresh_keys = jnp.moveaxis(key_new, 2, 0)
    fresh_values = jnp.moveaxis(value_new, 2, 0)
    attended = lax.map(one_head, (head_queries, head_keys, head_values, fresh_keys, fresh_values))
    attended = attended.reshape(KVH, REQS, NEW, G, HD).transpose(1, 2, 0, 3, 4).reshape(row_count, HQ * HD)
    residual = (values_in.reshape(row_count, D) + jnp.dot(attended, w_out, preferred_element_type=jnp.float32)).astype(jnp.bfloat16)
    normed = rms_norm(residual.astype(jnp.float32), mlp_gain).astype(jnp.bfloat16)
    gate_out = jnp.dot(normed, w_gate, preferred_element_type=jnp.float32)
    up_out = jnp.dot(normed, w_up, preferred_element_type=jnp.float32)
    activated = (jax.nn.silu(gate_out) * up_out).astype(jnp.bfloat16)
    down_out = jnp.dot(activated, w_down, preferred_element_type=jnp.float32)
    layer_out = (residual.astype(jnp.float32) + down_out).astype(jnp.bfloat16)
    return layer_out.reshape(REQS, NEW, D)
```

```python
import functools
import math

import jax
import jax.numpy as jnp
from jax import lax
from jax.experimental import pallas as pl
from jax.experimental.pallas import tpu as pltpu
from jax.sharding import PartitionSpec as P

EPSILON = 1e-05
NEGATIVE = -1e30
FLOOR = -1e20
ROPE_BASE = 500000.0
STRIDE = 32
SHORT_BLK = 4
ROWS = 16
UNROLL = 8
MESH = pl.DeviceIdType.MESH
F32 = jnp.float32
BF16 = jnp.bfloat16


def mm(a, b):
    return jnp.dot(a, b, preferred_element_type=F32)


def mm_t(a, b):
    return lax.dot_general(a, b, (((1,), (1,)), ((), ())), preferred_element_type=F32)


def layer_kernel(
    seqs, tens, n_long, others, req_dev, fresh, group, kv,
    ids, tok, gain1, gain2, cos, sin, wq, wk, wv, wo, wg, wu, wd, kc, vc,
    out,
    wq_v, wk_v, wv_v, wo_v, wg_v, wu_v, wd_v, kc_v, vc_v,
    nrm, qkv, qf, kf, vf, qs, ks, vs, so, sm, sl, ql, oo, om, ol, mj, pj, parts,
    att, s1, r1, own, s2, r2, res, act, s4, r4, s5, r5,
    w_sem, qsend, qrecv, psend, precv,
    s1_sem, r1_sem, s2_sem, r2_sem, s3_sem, r3_sem, s4_sem, r4_sem, s5_sem, r5_sem,
):
    s = lax.axis_index("seq")
    t = lax.axis_index("tensor")
    c = lax.rem(t, 2)
    x = t // 2
    xs = tens // 2
    step = STRIDE // req_dev
    rows, width = tok.shape
    bw = width // tens
    head = kc.shape[-1]
    page = kc.shape[2]
    scale = 1.0 / math.sqrt(head)
    mate = (s, t + 1 - 2 * c)
    lane_mask = functools.partial(lax.broadcasted_iota, jnp.int32)

    pairs = ((wq, wq_v), (wk, wk_v), (wv, wv_v), (kc, kc_v), (vc, vc_v), (wo, wo_v), (wg, wg_v), (wu, wu_v), (wd, wd_v))
    loads = [pltpu.make_async_copy(a, b, w_sem.at[i]) for i, (a, b) in enumerate(pairs)]
    for i in range(3):
        loads[i].start()

    barrier = pltpu.get_barrier_semaphore()
    for d in range(1, seqs):
        pl.semaphore_signal(barrier, inc=1, device_id=(lax.rem(s + d, seqs), t), device_id_type=MESH)
    pl.semaphore_signal(barrier, inc=1, device_id=mate, device_id_type=MESH)
    for d in range(1, xs):
        pl.semaphore_signal(barrier, inc=1, device_id=(s, lax.rem(x + d, xs) * 2 + c), device_id_type=MESH)

    loads[3].start()

    for i in range(rows // 16):
        v = tok[16 * i : 16 * i + 16, :].astype(F32)
        ms = jnp.mean(v * v, axis=-1, keepdims=True)
        nrm[16 * i : 16 * i + 16, :] = (v * lax.rsqrt(ms + EPSILON) * gain1[...].astype(F32)).astype(BF16)
    qf[...] = jnp.zeros_like(qf)
    kf[...] = jnp.zeros_like(kf)
    vf[...] = jnp.zeros_like(vf)

    def rope(v):
        return v * cos[...] + pltpu.roll(v, head // 2, 1) * sin[...]

    heads = kv * group
    loads[0].wait()
    loads[4].start()
    for lo in range(0, heads * head, 256):
        hi = min(lo + 256, heads * head)
        prod = mm(nrm[...], wq_v[:, lo:hi])
        for h in range(lo // head, hi // head):
            qkv[h] = rope(prod[:, h * head - lo : (h + 1) * head - lo])
    loads[1].wait()
    prod = mm(nrm[...], wk_v[...])
    for h in range(kv):
        qkv[heads + h] = rope(prod[:, h * head : (h + 1) * head])
    loads[2].wait()
    prod = mm(nrm[...], wv_v[...])
    for h in range(kv):
        qkv[heads + kv + h] = prod[:, h * head : (h + 1) * head]
    for n in range(fresh):
        src = pl.ds(n, req_dev, stride=fresh)
        for h in range(kv):
            for g in range(group):
                qf[h, pl.ds(g * fresh + n, req_dev, stride=ROWS), :] = qkv[h * group + g, src, :]
            kf[h, pl.ds(n, req_dev, stride=ROWS), :] = qkv[heads + h, src, :]
            vf[h, pl.ds(n, req_dev, stride=ROWS), :] = qkv[heads + kv + h, src, :]
    for h in range(kv):
        qs[h] = qf[h].astype(BF16)
        ks[h] = kf[h].astype(BF16)
        vs[h] = vf[h].astype(BF16)

    pl.semaphore_wait(barrier, seqs + xs - 1)
    is_home = lax.rem(s, step) == 0
    home = s // step

    def query_copy(d):
        return pltpu.make_async_remote_copy(
            src_ref=ql.at[home], dst_ref=ql.at[home], send_sem=qsend.at[d - 1], recv_sem=qrecv.at[home],
            device_id=(lax.rem(s + d, seqs), t), device_id_type=MESH,
        )

    @pl.when(is_home)
    def _():
        ql[home] = qs[:, :ROWS, :]
        for d in range(1, seqs):
            query_copy(d).start()

    loads[5].start()
    loads[6].start()
    loads[3].wait()
    loads[4].wait()

    def short_step(i, carry):
        for u in range(2):
            r = i * 2 + u
            base = pl.multiple_of(r * ROWS, ROWS)
            for h in range(kv):
                q = qs[h, pl.ds(base, ROWS), :]
                lane = lane_mask((ROWS, page), 1)
                tiles = []
                for b in range(SHORT_BLK):
                    slot = ids[0, r * SHORT_BLK + b]
                    count = ids[1, r * SHORT_BLK + b]
                    tiles.append(jnp.where(lane < count, mm_t(q, kc_v[slot, h]) * scale, NEGATIVE))
                token = lax.rem(lane_mask((ROWS, ROWS), 0), fresh)
                key = lane_mask((ROWS, ROWS), 1)
                fresh_s = jnp.where(key <= token, mm_t(q, ks[h, pl.ds(base, ROWS), :]) * scale, NEGATIVE)
                top = jnp.maximum(jnp.maximum(tiles[0], tiles[1]), jnp.maximum(tiles[2], tiles[3]))
                m = jnp.maximum(jnp.max(top, axis=1, keepdims=True), jnp.max(fresh_s, axis=1, keepdims=True))
                w_f = jnp.exp(fresh_s - m).astype(BF16)
                l = jnp.sum(w_f.astype(F32), axis=1, keepdims=True)
                o = mm(w_f, vs[h, pl.ds(base, ROWS), :])
                acc = None
                for b in range(SHORT_BLK):
                    w = jnp.exp(tiles[b] - m).astype(BF16)
                    o = o + mm(w, vc_v[ids[0, r * SHORT_BLK + b], h])
                    acc = w.astype(F32) if acc is None else acc + w.astype(F32)
                l = l + jnp.sum(acc, axis=1, keepdims=True)
                so[h, pl.ds(base, ROWS), :] = o
                sm[h, pl.ds(base, ROWS), :] = jnp.broadcast_to(m, (ROWS, head))
                sl[h, pl.ds(base, ROWS), :] = jnp.broadcast_to(l, (ROWS, head))
        return carry

    lax.fori_loop(0, req_dev // 2, short_step, 0)
    loads[7].start()
    loads[8].start()

    for j in range(n_long):
        @pl.when(s != j * step)
        def _():
            pltpu.make_async_remote_copy(
                src_ref=ql.at[j], dst_ref=ql.at[j], send_sem=qsend.at[0], recv_sem=qrecv.at[j],
                device_id=mate, device_id_type=MESH,
            ).wait_recv()

    first = req_dev * SHORT_BLK

    def long_step(i, carry):
        lane = lane_mask((ROWS, page), 1)
        scores = []
        for u in range(UNROLL):
            p = first + i * UNROLL + u
            for h in range(kv):
                value = mm_t(ql[ids[2, p], h], kc_v[ids[0, p], h]) * scale
                scores.append(jnp.where(lane < ids[1, p], value, NEGATIVE))
        tops = [jnp.max(v, axis=1, keepdims=True) for v in scores]
        for u in range(UNROLL):
            p = first + i * UNROLL + u
            for h in range(kv):
                v, m = scores[u * kv + h], tops[u * kv + h]
                w = jnp.where(lane < ids[1, p], jnp.exp(v - m), 0.0).astype(BF16)
                oo[i * UNROLL + u, h] = mm(w, vc_v[ids[0, p], h])
                om[i * UNROLL + u, h] = jnp.broadcast_to(m, (ROWS, head))
                ol[i * UNROLL + u, h] = jnp.broadcast_to(jnp.sum(w.astype(F32), axis=1, keepdims=True), (ROWS, head))
        return carry

    lax.fori_loop(0, others // UNROLL, long_step, 0)

    def top_step(i, carry):
        for u in range(4):
            p = i * 4 + u
            m = om[p]
            owner = ids[2, first + p]
            carry = tuple(jnp.maximum(carry[j], m + jnp.where(owner == j, 0.0, NEGATIVE)) for j in range(n_long))
        return carry

    floor = jnp.full((kv, ROWS, head), FLOOR, F32)
    tops = lax.fori_loop(0, others // 4, top_step, (floor,) * n_long)
    for j in range(n_long):
        mj[j] = tops[j]

    def sum_step(i, carry):
        sums, totals = carry
        for u in range(4):
            p = i * 4 + u
            owner = ids[2, first + p]
            e = jnp.exp(om[p] - mj[owner])
            o = e * oo[p]
            l = e * ol[p]
            marks = [jnp.where(owner == j, 1.0, 0.0) for j in range(n_long)]
            sums = tuple(sums[j] + marks[j] * o for j in range(n_long))
            totals = tuple(totals[j] + marks[j] * l for j in range(n_long))
        return sums, totals

    zero = jnp.zeros((kv, ROWS, head), F32)
    sums, totals = lax.fori_loop(0, others // 4, sum_step, ((zero,) * n_long, (zero,) * n_long))
    low = lane_mask((ROWS, head), 1) < head // 2
    for j in range(n_long):
        for h in range(kv):
            pj[j, h, 0] = sums[j][h]
            pj[j, h, 1] = jnp.where(low, tops[j][h], totals[j][h])

    def part_copy(j):
        return pltpu.make_async_remote_copy(
            src_ref=pj.at[j], dst_ref=parts.at[s], send_sem=psend.at[j], recv_sem=precv.at[s],
            device_id=(j * step, t), device_id_type=MESH,
        )

    for j in range(n_long):
        @pl.when(s != j * step)
        def _():
            part_copy(j).start()

    @pl.when(is_home)
    def _():
        for d in range(1, seqs):
            src = lax.rem(s + d, seqs)
            pltpu.make_async_remote_copy(
                src_ref=pj.at[0], dst_ref=parts.at[src], send_sem=psend.at[0], recv_sem=precv.at[src],
                device_id=mate, device_id_type=MESH,
            ).wait_recv()
        for h in range(kv):
            pieces = [(sm[h, :ROWS, :1], sl[h, :ROWS, :1], so[h, :ROWS, :])]
            blocks = [(pj[home, h, 0], pj[home, h, 1])]
            for d in range(1, seqs):
                src = lax.rem(s + d, seqs)
                blocks.append((parts[src, h, 0], parts[src, h, 1]))
            for o, ml in blocks:
                pieces.append((ml[:, :1], ml[:, head // 2 : head // 2 + 1], o))
            m = functools.reduce(jnp.maximum, [piece[0] for piece in pieces])
            l = jnp.zeros((ROWS, 1), F32)
            o = jnp.zeros((ROWS, head), F32)
            for m_i, l_i, o_i in pieces:
                e = jnp.exp(m_i - m)
                l = l + e * l_i
                o = o + e * o_i
            so[h, :ROWS, :] = o
            sl[h, :ROWS, :] = jnp.broadcast_to(l, (ROWS, head))

    for n in range(fresh):
        for h in range(kv):
            for g in range(group):
                src = pl.ds(g * fresh + n, req_dev, stride=ROWS)
                qkv[h * group + g, pl.ds(n, req_dev, stride=fresh), :] = so[h, src, :] / sl[h, src, :]
    for h in range(heads):
        att[:, h * head : (h + 1) * head] = qkv[h].astype(BF16)

    def to_mate(src, dst, send, recv):
        return pltpu.make_async_remote_copy(
            src_ref=src, dst_ref=dst, send_sem=send, recv_sem=recv, device_id=mate, device_id_type=MESH
        )

    def across(src, dst, send, recv, d):
        return pltpu.make_async_remote_copy(
            src_ref=src, dst_ref=dst, send_sem=send, recv_sem=recv,
            device_id=(s, lax.rem(x + d, xs) * 2 + c), device_id_type=MESH,
        )

    def block(ref, b):
        return ref[:, pl.ds(pl.multiple_of(b * bw, 128), bw)]

    loads[5].wait()
    started = []
    first_sum = [to_mate(s1.at[k], r1.at[k], s1_sem.at[k], r1_sem.at[k]) for k in range(xs)]
    for k in range(xs):
        s1[k] = mm(att[...], block(wo_v, (1 - c) * xs + k)).astype(BF16)
        first_sum[k].start()
    for k in range(xs):
        own[k] = mm(att[...], block(wo_v, c * xs + k))
    crossing = {}
    for k in range(xs):
        first_sum[k].wait_recv()
        total = own[k] + r1[k].astype(F32)
        own[k] = total
        s2[k] = total.astype(BF16)
        for d in range(1, xs):
            crossing[k, d] = across(s2.at[k], r2.at[d - 1, k], s2_sem.at[d - 1, k], r2_sem.at[d - 1, k], d)
            crossing[k, d].start()
    spread = []
    for k in range(xs):
        b = c * xs + k
        total = block(tok, b).astype(F32) + own[k]
        for d in range(1, xs):
            crossing[k, d].wait_recv()
            total = total + r2[d - 1, k].astype(F32)
        res[b] = total.astype(BF16)
        copy = to_mate(res.at[b], res.at[b], s3_sem.at[k], r3_sem.at[k])
        copy.start()
        spread.append(copy)
    for k in range(xs):
        b = (1 - c) * xs + k
        to_mate(res.at[b], res.at[b], s3_sem.at[k], r3_sem.at[k]).wait_recv()

    square = jnp.zeros((rows, 1), F32)
    for b in range(tens):
        v = res[b].astype(F32)
        square = square + jnp.sum(v * v, axis=-1, keepdims=True)
    inverse = lax.rsqrt(square / width + EPSILON)
    for b in range(tens):
        cols = slice(b * bw, (b + 1) * bw)
        nrm[:, cols] = (res[b].astype(F32) * inverse * gain2[:, cols].astype(F32)).astype(BF16)

    loads[6].wait()
    loads[7].wait()
    for lo in range(0, act.shape[1], 256):
        gate = mm(nrm[...], wg_v[:, lo : lo + 256])
        up = mm(nrm[...], wu_v[:, lo : lo + 256])
        act[:, lo : lo + 256] = (gate / (1.0 + jnp.exp(-gate)) * up).astype(BF16)

    loads[8].wait()
    pair_sum = []
    for k in range(xs):
        to = lax.rem(x + 1 + k, xs)
        s4[k] = mm(act[...], block(wd_v, to * 2 + 1 - c)).astype(BF16)
        copy = to_mate(s4.at[k], r4.at[k], s4_sem.at[k], r4_sem.at[k])
        copy.start()
        pair_sum.append(copy)
    last = []
    for k in range(xs):
        to = lax.rem(x + 1 + k, xs)
        total = mm(act[...], block(wd_v, to * 2 + c))
        pair_sum[k].wait_recv()
        total = total + r4[k].astype(F32)
        if k < xs - 1:
            s5[k] = total.astype(BF16)
            copy = across(s5.at[k], r5.at[k], s5_sem.at[k], r5_sem.at[k], k + 1)
            copy.start()
            last.append(copy)
        else:
            total = total + res[t].astype(F32)
            for copy, d in zip(last, range(xs)):
                copy.wait_recv()
                total = total + r5[d].astype(F32)
            out[...] = total.astype(BF16)

    @pl.when(is_home)
    def _():
        for d in range(1, seqs):
            query_copy(d).wait_send()

    for j in range(n_long):
        @pl.when(s != j * step)
        def _():
            part_copy(j).wait_send()

    for copy in first_sum + list(crossing.values()) + spread + pair_sum + last:
        copy.wait_send()


def per_device(
    tokens, lengths, page_request, page_block, k_cache, v_cache, attn_gain, w_query, w_key, w_value,
    w_out, mlp_gain, w_gate, w_up, w_down,
):
    req_dev, fresh, width = tokens.shape
    slots, kv, page, head = k_cache.shape
    group = w_query.shape[1] // (kv * head)
    rows = req_dev * fresh
    seqs, tens = lax.axis_size("seq"), lax.axis_size("tensor")
    xs = tens // 2
    bw = width // tens
    requests = lengths.shape[0]
    n_long = requests // STRIDE
    hidden = w_gate.shape[1]
    home_row = lax.axis_index("seq") * req_dev

    own_length = lax.dynamic_slice_in_dim(lengths, home_row, req_dev)
    position = (own_length[:, None] + jnp.arange(fresh, dtype=jnp.int32)[None, :]).reshape(rows, 1)
    half = head // 2
    inverse = 1.0 / ROPE_BASE ** (jnp.arange(half, dtype=F32) * 2.0 / head)
    angle = position.astype(F32) * jnp.concatenate([inverse, inverse])[None, :]
    sign = jnp.where(jnp.arange(head) < half, -1.0, 1.0)
    cosine = jnp.cos(angle)
    sine = jnp.sin(angle) * sign[None, :]

    is_short = (page_request % STRIDE != 0) & (page_block < SHORT_BLK)
    index = jnp.arange(slots, dtype=jnp.int32)
    before = index[None, :] < index[:, None]
    rank = jnp.sum(jnp.where(before & ~is_short[None, :], 1, 0), axis=1)
    first = req_dev * SHORT_BLK
    place = jnp.where(is_short, (page_request - home_row) * SHORT_BLK + page_block, first + rank)
    most = slots - first + SHORT_BLK * -(-req_dev // STRIDE)
    others = -(-most // UNROLL) * UNROLL
    total = -(-(first + others) // 128) * 128
    owner_length = jnp.sum(
        jnp.where(page_request[:, None] == jnp.arange(requests, dtype=jnp.int32)[None, :], lengths[None, :], 0), axis=1
    )
    count = jnp.clip(owner_length - page_block * page, 0, page)
    table = jnp.stack([index, count, page_request // STRIDE])
    at = place[None, :] == jnp.arange(total, dtype=jnp.int32)[:, None]
    ids = jnp.sum(jnp.where(at[None], table[:, None, :], 0), axis=2)

    vm = lambda shape, dtype=F32: pltpu.VMEM(shape, dtype)
    dma = lambda *shape: pltpu.SemaphoreType.DMA(shape)
    whole = pl.BlockSpec(memory_space=pltpu.VMEM)
    stay = pl.BlockSpec(memory_space=pl.ANY)
    big = (w_query, w_key, w_value, w_out, w_gate, w_up, w_down, k_cache, v_cache)
    tall = (kv, req_dev * ROWS, head)
    scratch = [vm(a.shape, BF16) for a in big]
    scratch += [
        vm((rows, width), BF16), vm((kv * (group + 2), rows, head)), vm(tall), vm(tall), vm(tall),
        vm(tall, BF16), vm(tall, BF16), vm(tall, BF16), vm(tall), vm(tall), vm(tall),
        vm((n_long, kv, ROWS, head), BF16),
        vm((others, kv, ROWS, head)), vm((others, kv, ROWS, head)), vm((others, kv, ROWS, head)),
        vm((n_long, kv, ROWS, head)), vm((n_long, kv, 2, ROWS, head)), vm((seqs, kv, 2, ROWS, head)),
        vm((rows, kv * group * head), BF16),
        vm((xs, rows, bw), BF16), vm((xs, rows, bw), BF16), vm((xs, rows, bw)),
        vm((xs, rows, bw), BF16), vm((xs - 1, xs, rows, bw), BF16), vm((tens, rows, bw), BF16),
        vm((rows, hidden), BF16),
        vm((xs, rows, bw), BF16), vm((xs, rows, bw), BF16), vm((xs - 1, rows, bw), BF16), vm((xs - 1, rows, bw), BF16),
        dma(9), dma(seqs - 1), dma(n_long), dma(n_long), dma(seqs),
        dma(xs), dma(xs), dma(xs - 1, xs), dma(xs - 1, xs), dma(xs), dma(xs), dma(xs), dma(xs), dma(xs - 1), dma(xs - 1),
    ]
    moved = sum(a.size for a in big) * 2
    out = pl.pallas_call(
        functools.partial(layer_kernel, seqs, tens, n_long, others, req_dev, fresh, group, kv),
        out_shape=jax.ShapeDtypeStruct((rows, bw), BF16),
        in_specs=[pl.BlockSpec(memory_space=pltpu.SMEM)] + [whole] * 5 + [stay] * 9,
        out_specs=whole,
        scratch_shapes=scratch,
        compiler_params=pltpu.CompilerParams(
            collective_id=0, has_side_effects=True, vmem_limit_bytes=60 * 1024 * 1024
        ),
        cost_estimate=pl.CostEstimate(flops=2 * rows * moved, bytes_accessed=moved, transcendentals=0),
        name="layer",
    )(
        ids, tokens.reshape(rows, width), attn_gain.reshape(1, width), mlp_gain.reshape(1, width),
        cosine, sine, *big,
    )
    return out.reshape(req_dev, fresh, bw)


def solution(mesh):
    placed = (
        P("seq", None, None),
        P(),
        P("seq"),
        P("seq"),
        P("seq", "tensor", None, None),
        P("seq", "tensor", None, None),
        P(),
        P(None, "tensor"),
        P(None, "tensor"),
        P(None, "tensor"),
        P("tensor", None),
        P(),
        P(None, "tensor"),
        P(None, "tensor"),
        P("tensor", None),
    )
    return jax.shard_map(
        per_device, mesh=mesh, in_specs=placed, out_specs=P("seq", None, "tensor"), check_vma=False
    )
```

```python
import functools
import math

import jax
import jax.numpy as jnp
import numpy as np
from jax import lax
from jax.experimental import pallas as pl
from jax.experimental.pallas import tpu as pltpu
from jax.sharding import PartitionSpec as P

EPSILON = 1e-05
NEGATIVE = -1e30
FLOOR = -1e20
ROPE_BASE = 500000.0
STRIDE = 32
SHORT_BLK = 4
ROWS = 16
UNROLL = 12
SHORT_UNROLL = 4
MESH = pl.DeviceIdType.MESH
F32 = jnp.float32
BF16 = jnp.bfloat16


def mm(a, b):
    return jnp.dot(a, b, preferred_element_type=F32)


def mm_t(a, b):
    return lax.dot_general(a, b, (((1,), (1,)), ((), ())), preferred_element_type=F32)


def layer_kernel(
    seqs, tens, n_long, others, req_dev, fresh, group, kv,
    places, lengths, page_request, page_block, tok, gain1, gain2, freq, wq, wk, wv, wo, wg, wu, wd, kc, vc,
    out,
    wq_v, wk_v, wv_v, wo_v, wg_v, wu_v, wd_v, kc_v, vc_v,
    xf, cos, sin, nrm, qkv, qf, kf, vf, qs, ks, vs, so, sm, sl, ql, oo, om, ol, mj, pj, parts,
    att, s1, r1, own, s2, r2, res, act, s4, r4, s5, r5,
    w_sem, qsend, qrecv, psend, precv,
    s1_sem, r1_sem, s2_sem, r2_sem, s3_sem, r3_sem, s4_sem, r4_sem, s5_sem, r5_sem,
):
    s = lax.axis_index("seq")
    t = lax.axis_index("tensor")
    c = lax.rem(t, 2)
    x = t // 2
    xs = tens // 2
    step = STRIDE // req_dev
    rows, width = xf.shape
    bw = width // tens
    head = kc.shape[-1]
    page = kc.shape[2]
    scale = 1.0 / math.sqrt(head)
    mate = (s, t + 1 - 2 * c)
    lane_mask = functools.partial(lax.broadcasted_iota, jnp.int32)

    pairs = ((wq, wq_v), (wk, wk_v), (wv, wv_v), (kc, kc_v), (vc, vc_v), (wo, wo_v), (wg, wg_v), (wu, wu_v), (wd, wd_v))
    loads = [pltpu.make_async_copy(a, b, w_sem.at[i]) for i, (a, b) in enumerate(pairs)]
    for i in range(3):
        loads[i].start()

    barrier = pltpu.get_barrier_semaphore()
    for d in range(1, seqs):
        pl.semaphore_signal(barrier, inc=1, device_id=(lax.rem(s + d, seqs), t), device_id_type=MESH)
    pl.semaphore_signal(barrier, inc=1, device_id=mate, device_id_type=MESH)
    for d in range(1, xs):
        pl.semaphore_signal(barrier, inc=1, device_id=(s, lax.rem(x + d, xs) * 2 + c), device_id_type=MESH)

    loads[3].start()

    for r in range(req_dev):
        xf[fresh * r : fresh * r + fresh, :] = tok[r].astype(F32)
    for i in range(rows // 16):
        v = xf[16 * i : 16 * i + 16, :]
        ms = jnp.mean(v * v, axis=-1, keepdims=True)
        nrm[16 * i : 16 * i + 16, :] = (v * lax.rsqrt(ms + EPSILON) * gain1[...].astype(F32).reshape(1, width)).astype(BF16)
    qf[...] = jnp.zeros_like(qf)
    kf[...] = jnp.zeros_like(kf)
    vf[...] = jnp.zeros_like(vf)

    row = lane_mask((rows, head), 0)
    position = lax.rem(row, fresh)
    for r in range(req_dev):
        position = position + jnp.where(row // fresh == r, lengths[s * req_dev + r], 0)
    angle = position.astype(F32) * freq[...]
    cos[...] = jnp.cos(angle)
    sin[...] = jnp.where(lane_mask((rows, head), 1) < head // 2, -1.0, 1.0) * jnp.sin(angle)

    def rope(v):
        return v * cos[...] + pltpu.roll(v, head // 2, 1) * sin[...]

    heads = kv * group
    loads[0].wait()
    loads[4].start()
    for lo in range(0, heads * head, 256):
        hi = min(lo + 256, heads * head)
        prod = mm(nrm[...], wq_v[:, lo:hi])
        for h in range(lo // head, hi // head):
            qkv[h] = rope(prod[:, h * head - lo : (h + 1) * head - lo])
    loads[1].wait()
    prod = mm(nrm[...], wk_v[...])
    for h in range(kv):
        qkv[heads + h] = rope(prod[:, h * head : (h + 1) * head])
    loads[2].wait()
    prod = mm(nrm[...], wv_v[...])
    for h in range(kv):
        qkv[heads + kv + h] = prod[:, h * head : (h + 1) * head]
    for n in range(fresh):
        src = pl.ds(n, req_dev, stride=fresh)
        for h in range(kv):
            for g in range(group):
                qf[h, pl.ds(g * fresh + n, req_dev, stride=ROWS), :] = qkv[h * group + g, src, :]
            kf[h, pl.ds(n, req_dev, stride=ROWS), :] = qkv[heads + h, src, :]
            vf[h, pl.ds(n, req_dev, stride=ROWS), :] = qkv[heads + kv + h, src, :]
    for h in range(kv):
        qs[h] = qf[h].astype(BF16)
        ks[h] = kf[h].astype(BF16)
        vs[h] = vf[h].astype(BF16)

    pl.semaphore_wait(barrier, seqs + xs - 1)
    is_home = lax.rem(s, step) == 0
    home = s // step

    def query_copy(d):
        return pltpu.make_async_remote_copy(
            src_ref=ql.at[home], dst_ref=ql.at[home], send_sem=qsend.at[d - 1], recv_sem=qrecv.at[home],
            device_id=(lax.rem(s + d, seqs), t), device_id_type=MESH,
        )

    @pl.when(is_home)
    def _():
        ql[home] = qs[:, :ROWS, :]
        for d in range(1, seqs):
            query_copy(d).start()

    loads[5].start()
    loads[6].start()
    loads[3].wait()
    loads[4].wait()

    def entry(p):
        known = places[p] - 1
        slot = jnp.maximum(known, 0)
        request = page_request[slot]
        used = jnp.where(known < 0, 0, lengths[request] - page_block[slot] * page)
        return slot, used, request // STRIDE

    def short_step(i, carry):
        lane = lane_mask((ROWS, page), 1)
        token = lax.rem(lane_mask((ROWS, ROWS), 0), fresh)
        key = lane_mask((ROWS, ROWS), 1)
        for u in range(SHORT_UNROLL):
            r = i * SHORT_UNROLL + u
            span = pl.ds(pl.multiple_of(r * ROWS, ROWS), ROWS)
            entries = [entry(r * SHORT_BLK + b) for b in range(SHORT_BLK)]
            weights = []
            for h in range(kv):
                q = qs[h, span, :]
                keys = jnp.concatenate([kc_v[slot, h] for slot, _, _ in entries], axis=0)
                value = mm_t(q, keys) * scale
                tiles = [
                    jnp.where(lane < used, value[:, b * page : (b + 1) * page], NEGATIVE)
                    for b, (_, used, _) in enumerate(entries)
                ]
                fresh_s = jnp.where(key <= token, mm_t(q, ks[h, span, :]) * scale, NEGATIVE)
                top = functools.reduce(jnp.maximum, tiles)
                m = jnp.maximum(jnp.max(top, axis=1, keepdims=True), jnp.max(fresh_s, axis=1, keepdims=True))
                w_f = jnp.exp(fresh_s - m).astype(BF16)
                w = [jnp.exp(tile - m).astype(BF16) for tile in tiles]
                l = jnp.sum(w_f.astype(F32), axis=1, keepdims=True)
                l = l + jnp.sum(sum(part.astype(F32) for part in w), axis=1, keepdims=True)
                so[h, span, :] = mm(w_f, vs[h, span, :])
                sm[h, span, :] = jnp.broadcast_to(m, (ROWS, head))
                sl[h, span, :] = jnp.broadcast_to(l, (ROWS, head))
                weights.append(jnp.concatenate(w, axis=1))
            values = jnp.concatenate(
                [jnp.concatenate([vc_v[slot, h] for h in range(kv)], axis=1) for slot, _, _ in entries], axis=0
            )
            o = mm(jnp.concatenate(weights, axis=0), values)
            for h in range(kv):
                so[h, span, :] += o[h * ROWS : (h + 1) * ROWS, h * head : (h + 1) * head]
        return carry

    lax.fori_loop(0, req_dev // SHORT_UNROLL, short_step, 0)
    loads[7].start()
    loads[8].start()

    for j in range(n_long):
        @pl.when(s != j * step)
        def _():
            pltpu.make_async_remote_copy(
                src_ref=ql.at[j], dst_ref=ql.at[j], send_sem=qsend.at[0], recv_sem=qrecv.at[j],
                device_id=mate, device_id_type=MESH,
            ).wait_recv()

    first = req_dev * SHORT_BLK

    def long_step(i, carry):
        lane = lane_mask((ROWS, page), 1)
        entries = [entry(first + i * UNROLL + u) for u in range(UNROLL)]
        places_of = [(u, h) for u in range(UNROLL) for h in range(kv)]
        pairs_of = [places_of[n : n + 2] for n in range(0, len(places_of), 2)]
        scores = []
        for pair in pairs_of:
            q = jnp.concatenate([ql[entries[u][2], h] for u, h in pair], axis=0)
            keys = jnp.concatenate([kc_v[entries[u][0], h] for u, h in pair], axis=0)
            value = mm_t(q, keys) * scale
            for n, (u, _) in enumerate(pair):
                part = value[n * ROWS : (n + 1) * ROWS, n * page : (n + 1) * page]
                scores.append(jnp.where(lane < entries[u][1], part, NEGATIVE))
        tops = [jnp.max(v, axis=1, keepdims=True) for v in scores]
        for k, pair in enumerate(pairs_of):
            weights = []
            for n, (u, h) in enumerate(pair):
                v, m = scores[2 * k + n], tops[2 * k + n]
                w = jnp.where(lane < entries[u][1], jnp.exp(v - m), 0.0).astype(BF16)
                om[i * UNROLL + u, h] = jnp.broadcast_to(m, (ROWS, head))
                ol[i * UNROLL + u, h] = jnp.broadcast_to(jnp.sum(w.astype(F32), axis=1, keepdims=True), (ROWS, head))
                weights.append(w)
            values = jnp.concatenate([vc_v[entries[u][0], h] for u, h in pair], axis=1)
            o = mm(jnp.concatenate(weights, axis=0), values)
            for n, (u, h) in enumerate(pair):
                oo[i * UNROLL + u, h] = o[n * ROWS : (n + 1) * ROWS, n * head : (n + 1) * head]
        return carry

    lax.fori_loop(0, others // UNROLL, long_step, 0)

    def top_step(i, carry):
        for u in range(4):
            p = i * 4 + u
            m = om[p]
            owner = entry(first + p)[2]
            carry = tuple(jnp.maximum(carry[j], m + jnp.where(owner == j, 0.0, NEGATIVE)) for j in range(n_long))
        return carry

    floor = jnp.full((kv, ROWS, head), FLOOR, F32)
    tops = lax.fori_loop(0, others // 4, top_step, (floor,) * n_long)
    for j in range(n_long):
        mj[j] = tops[j]

    def sum_step(i, carry):
        sums, totals = carry
        for u in range(4):
            p = i * 4 + u
            owner = entry(first + p)[2]
            e = jnp.exp(om[p] - mj[owner])
            o = e * oo[p]
            l = e * ol[p]
            marks = [jnp.where(owner == j, 1.0, 0.0) for j in range(n_long)]
            sums = tuple(sums[j] + marks[j] * o for j in range(n_long))
            totals = tuple(totals[j] + marks[j] * l for j in range(n_long))
        return sums, totals

    zero = jnp.zeros((kv, ROWS, head), F32)
    sums, totals = lax.fori_loop(0, others // 4, sum_step, ((zero,) * n_long, (zero,) * n_long))
    low = lane_mask((ROWS, head), 1) < head // 2
    for j in range(n_long):
        for h in range(kv):
            pj[j, h, 0] = sums[j][h]
            pj[j, h, 1] = jnp.where(low, tops[j][h], totals[j][h])

    def part_copy(j):
        return pltpu.make_async_remote_copy(
            src_ref=pj.at[j], dst_ref=parts.at[s], send_sem=psend.at[j], recv_sem=precv.at[s],
            device_id=(j * step, t), device_id_type=MESH,
        )

    for j in range(n_long):
        @pl.when(s != j * step)
        def _():
            part_copy(j).start()

    @pl.when(is_home)
    def _():
        for d in range(1, seqs):
            src = lax.rem(s + d, seqs)
            pltpu.make_async_remote_copy(
                src_ref=pj.at[0], dst_ref=parts.at[src], send_sem=psend.at[0], recv_sem=precv.at[src],
                device_id=mate, device_id_type=MESH,
            ).wait_recv()
        for h in range(kv):
            pieces = [(sm[h, :ROWS, :1], sl[h, :ROWS, :1], so[h, :ROWS, :])]
            blocks = [(pj[home, h, 0], pj[home, h, 1])]
            for d in range(1, seqs):
                src = lax.rem(s + d, seqs)
                blocks.append((parts[src, h, 0], parts[src, h, 1]))
            for o, ml in blocks:
                pieces.append((ml[:, :1], ml[:, head // 2 : head // 2 + 1], o))
            m = functools.reduce(jnp.maximum, [piece[0] for piece in pieces])
            l = jnp.zeros((ROWS, 1), F32)
            o = jnp.zeros((ROWS, head), F32)
            for m_i, l_i, o_i in pieces:
                e = jnp.exp(m_i - m)
                l = l + e * l_i
                o = o + e * o_i
            so[h, :ROWS, :] = o
            sl[h, :ROWS, :] = jnp.broadcast_to(l, (ROWS, head))

    for n in range(fresh):
        for h in range(kv):
            for g in range(group):
                src = pl.ds(g * fresh + n, req_dev, stride=ROWS)
                qkv[h * group + g, pl.ds(n, req_dev, stride=fresh), :] = so[h, src, :] / sl[h, src, :]
    for h in range(heads):
        att[:, h * head : (h + 1) * head] = qkv[h].astype(BF16)

    def to_mate(src, dst, send, recv):
        return pltpu.make_async_remote_copy(
            src_ref=src, dst_ref=dst, send_sem=send, recv_sem=recv, device_id=mate, device_id_type=MESH
        )

    def across(src, dst, send, recv, d):
        return pltpu.make_async_remote_copy(
            src_ref=src, dst_ref=dst, send_sem=send, recv_sem=recv,
            device_id=(s, lax.rem(x + d, xs) * 2 + c), device_id_type=MESH,
        )

    def block(ref, b):
        return ref[:, pl.ds(pl.multiple_of(b * bw, 128), bw)]

    loads[5].wait()
    started = []
    first_sum = [to_mate(s1.at[k], r1.at[k], s1_sem.at[k], r1_sem.at[k]) for k in range(xs)]
    for k in range(xs):
        s1[k] = mm(att[...], block(wo_v, (1 - c) * xs + k)).astype(BF16)
        first_sum[k].start()
    for k in range(xs):
        own[k] = mm(att[...], block(wo_v, c * xs + k))
    crossing = {}
    for k in range(xs):
        first_sum[k].wait_recv()
        total = own[k] + r1[k].astype(F32)
        own[k] = total
        s2[k] = total.astype(BF16)
        for d in range(1, xs):
            crossing[k, d] = across(s2.at[k], r2.at[d - 1, k], s2_sem.at[d - 1, k], r2_sem.at[d - 1, k], d)
            crossing[k, d].start()
    spread = []
    for k in range(xs):
        b = c * xs + k
        total = block(xf, b) + own[k]
        for d in range(1, xs):
            crossing[k, d].wait_recv()
            total = total + r2[d - 1, k].astype(F32)
        res[b] = total.astype(BF16)
        copy = to_mate(res.at[b], res.at[b], s3_sem.at[k], r3_sem.at[k])
        copy.start()
        spread.append(copy)
    for k in range(xs):
        b = (1 - c) * xs + k
        to_mate(res.at[b], res.at[b], s3_sem.at[k], r3_sem.at[k]).wait_recv()

    square = jnp.zeros((rows, 1), F32)
    for b in range(tens):
        v = res[b].astype(F32)
        square = square + jnp.sum(v * v, axis=-1, keepdims=True)
    inverse = lax.rsqrt(square / width + EPSILON)
    scales = gain2[...].astype(F32).reshape(1, width)
    for b in range(tens):
        cols = slice(b * bw, (b + 1) * bw)
        nrm[:, cols] = (res[b].astype(F32) * inverse * scales[:, cols]).astype(BF16)

    loads[6].wait()
    loads[7].wait()
    for lo in range(0, act.shape[1], 256):
        gate = mm(nrm[...], wg_v[:, lo : lo + 256])
        up = mm(nrm[...], wu_v[:, lo : lo + 256])
        act[:, lo : lo + 256] = (gate / (1.0 + jnp.exp(-gate)) * up).astype(BF16)

    loads[8].wait()
    pair_sum = []
    for k in range(xs):
        to = lax.rem(x + 1 + k, xs)
        s4[k] = mm(act[...], block(wd_v, to * 2 + 1 - c)).astype(BF16)
        copy = to_mate(s4.at[k], r4.at[k], s4_sem.at[k], r4_sem.at[k])
        copy.start()
        pair_sum.append(copy)
    last = []
    for k in range(xs):
        to = lax.rem(x + 1 + k, xs)
        total = mm(act[...], block(wd_v, to * 2 + c))
        pair_sum[k].wait_recv()
        total = total + r4[k].astype(F32)
        if k < xs - 1:
            s5[k] = total.astype(BF16)
            copy = across(s5.at[k], r5.at[k], s5_sem.at[k], r5_sem.at[k], k + 1)
            copy.start()
            last.append(copy)
        else:
            total = total + res[t].astype(F32)
            for copy, d in zip(last, range(xs)):
                copy.wait_recv()
                total = total + r5[d].astype(F32)
            for r in range(req_dev):
                out[r] = total[fresh * r : fresh * r + fresh].astype(BF16)

    @pl.when(is_home)
    def _():
        for d in range(1, seqs):
            query_copy(d).wait_send()

    for j in range(n_long):
        @pl.when(s != j * step)
        def _():
            part_copy(j).wait_send()

    for copy in first_sum + list(crossing.values()) + spread + pair_sum + last:
        copy.wait_send()


def per_device(
    tokens, lengths, page_request, page_block, k_cache, v_cache, attn_gain, w_query, w_key, w_value,
    w_out, mlp_gain, w_gate, w_up, w_down,
):
    req_dev, fresh, width = tokens.shape
    slots, kv, page, head = k_cache.shape
    group = w_query.shape[1] // (kv * head)
    rows = req_dev * fresh
    seqs, tens = lax.axis_size("seq"), lax.axis_size("tensor")
    xs = tens // 2
    bw = width // tens
    n_long = lengths.shape[0] // STRIDE
    hidden = w_gate.shape[1]
    home_row = lax.axis_index("seq") * req_dev

    inverse = ROPE_BASE ** (-np.arange(head // 2) * 2.0 / head)
    freq = np.concatenate([inverse, inverse])[None, :].astype(np.float32)

    first = req_dev * SHORT_BLK
    most = slots - first + SHORT_BLK * -(-req_dev // STRIDE)
    others = -(-most // UNROLL) * UNROLL

    is_short = (page_request % STRIDE != 0) & (page_block < SHORT_BLK)
    code = jnp.where(is_short, (page_request - home_row) * SHORT_BLK + page_block + 1, 0)
    line = lax.broadcasted_iota(jnp.int32, (slots, slots), 0)
    index = lax.broadcasted_iota(jnp.int32, (slots, slots), 1)
    rank = jnp.sum(jnp.where(jnp.maximum(code[None, :], index - line + 1) <= 0, 1, 0), axis=1)
    line = lax.broadcasted_iota(jnp.int32, (first + others, slots), 0)
    index = lax.broadcasted_iota(jnp.int32, (first + others, slots), 1)
    is_place = (code[None, :] - (line + 1) == 0) | (
        jnp.maximum(jnp.abs(rank[None, :] + (first - line)), code[None, :]) == 0
    )
    places = jnp.sum(jnp.where(is_place, index + 1, 0), axis=1)

    vm = lambda shape, dtype=F32: pltpu.VMEM(shape, dtype)
    dma = lambda *shape: pltpu.SemaphoreType.DMA(shape)
    whole = pl.BlockSpec(memory_space=pltpu.VMEM)
    stay = pl.BlockSpec(memory_space=pl.ANY)
    big = (w_query, w_key, w_value, w_out, w_gate, w_up, w_down, k_cache, v_cache)
    tall = (kv, req_dev * ROWS, head)
    scratch = [vm(a.shape, BF16) for a in big]
    scratch += [
        vm((rows, width)), vm((rows, head)), vm((rows, head)), vm((rows, width), BF16), vm((kv * (group + 2), rows, head)), vm(tall), vm(tall), vm(tall),
        vm(tall, BF16), vm(tall, BF16), vm(tall, BF16), vm(tall), vm(tall), vm(tall),
        vm((n_long, kv, ROWS, head), BF16),
        vm((others, kv, ROWS, head)), vm((others, kv, ROWS, head)), vm((others, kv, ROWS, head)),
        vm((n_long, kv, ROWS, head)), vm((n_long, kv, 2, ROWS, head)), vm((seqs, kv, 2, ROWS, head)),
        vm((rows, kv * group * head), BF16),
        vm((xs, rows, bw), BF16), vm((xs, rows, bw), BF16), vm((xs, rows, bw)),
        vm((xs, rows, bw), BF16), vm((xs - 1, xs, rows, bw), BF16), vm((tens, rows, bw), BF16),
        vm((rows, hidden), BF16),
        vm((xs, rows, bw), BF16), vm((xs, rows, bw), BF16), vm((xs - 1, rows, bw), BF16), vm((xs - 1, rows, bw), BF16),
        dma(9), dma(seqs - 1), dma(n_long), dma(n_long), dma(seqs),
        dma(xs), dma(xs), dma(xs - 1, xs), dma(xs - 1, xs), dma(xs), dma(xs), dma(xs), dma(xs), dma(xs - 1), dma(xs - 1),
    ]
    moved = sum(a.size for a in big) * 2
    out = pl.pallas_call(
        functools.partial(layer_kernel, seqs, tens, n_long, others, req_dev, fresh, group, kv),
        out_shape=jax.ShapeDtypeStruct((req_dev, fresh, bw), BF16),
        in_specs=[pl.BlockSpec(memory_space=pltpu.SMEM)] * 4 + [whole] * 4 + [stay] * 9,
        out_specs=whole,
        scratch_shapes=scratch,
        compiler_params=pltpu.CompilerParams(
            collective_id=0, has_side_effects=True, vmem_limit_bytes=60 * 1024 * 1024
        ),
        cost_estimate=pl.CostEstimate(flops=2 * rows * moved, bytes_accessed=moved, transcendentals=0),
        name="layer",
    )(
        places, lengths, page_request, page_block, tokens, attn_gain, mlp_gain, freq, *big,
    )
    return out


def solution(mesh):
    placed = (
        P("seq", None, None),
        P(),
        P("seq"),
        P("seq"),
        P("seq", "tensor", None, None),
        P("seq", "tensor", None, None),
        P(),
        P(None, "tensor"),
        P(None, "tensor"),
        P(None, "tensor"),
        P("tensor", None),
        P(),
        P(None, "tensor"),
        P(None, "tensor"),
        P("tensor", None),
    )
    return jax.shard_map(
        per_device, mesh=mesh, in_specs=placed, out_specs=P("seq", None, "tensor"), check_vma=False
    )
```

```python
import functools
import math

import jax
import jax.numpy as jnp
import numpy as np
from jax import lax
from jax.experimental import pallas as pl
from jax.experimental.pallas import tpu as pltpu
from jax.sharding import PartitionSpec as P

EPSILON = 1e-05
NEGATIVE = -1e30
FLOOR = -1e20
ROPE_BASE = 500000.0
STRIDE = 32
SHORT_BLK = 4
ROWS = 16
UNROLL = 12
SHORT_UNROLL = 4
SHORT_FIRST = 1
MESH = pl.DeviceIdType.MESH
F32 = jnp.float32
BF16 = jnp.bfloat16


def mm(a, b):
    return jnp.dot(a, b, preferred_element_type=F32)


def mm_t(a, b):
    return lax.dot_general(a, b, (((1,), (1,)), ((), ())), preferred_element_type=F32)


def layer_kernel(
    seqs, tens, n_long, others, req_dev, fresh, group, kv,
    places, lengths, page_request, page_block, tok, gain1, gain2, freq, wq, wk, wv, wo, wg, wu, wd, kc, vc,
    out,
    wq_v, wk_v, wv_v, wo_v, wg_v, wu_v, wd_v, kc_v, vc_v,
    xf, cos, sin, nrm, qkv, qf, kf, vf, qs, ks, vs, so, sm, sl, ql, oo, om, ol, mj, pj, parts,
    att, s1, r1, own, s2, r2, res, scales, gates, ups, act, s4, r4, s5, r5,
    w_sem, qsend, qrecv, psend, precv,
    s1_sem, r1_sem, s2_sem, r2_sem, s3_sem, r3_sem, s4_sem, r4_sem, s5_sem, r5_sem,
):
    s = lax.axis_index("seq")
    t = lax.axis_index("tensor")
    c = lax.rem(t, 2)
    x = t // 2
    xs = tens // 2
    step = STRIDE // req_dev
    rows, width = xf.shape
    bw = width // tens
    head = kc.shape[-1]
    page = kc.shape[2]
    scale = 1.0 / math.sqrt(head)
    mate = (s, t + 1 - 2 * c)
    lane_mask = functools.partial(lax.broadcasted_iota, jnp.int32)

    pairs = ((wq, wq_v), (wk, wk_v), (wv, wv_v), (kc, kc_v), (vc, vc_v), (wo, wo_v), (wg, wg_v), (wu, wu_v), (wd, wd_v))
    loads = [pltpu.make_async_copy(a, b, w_sem.at[i]) for i, (a, b) in enumerate(pairs)]
    for i in range(3):
        loads[i].start()

    barrier = pltpu.get_barrier_semaphore()
    for d in range(1, seqs):
        pl.semaphore_signal(barrier, inc=1, device_id=(lax.rem(s + d, seqs), t), device_id_type=MESH)
    pl.semaphore_signal(barrier, inc=1, device_id=mate, device_id_type=MESH)
    for d in range(1, xs):
        pl.semaphore_signal(barrier, inc=1, device_id=(s, lax.rem(x + d, xs) * 2 + c), device_id_type=MESH)

    for r in range(req_dev):
        xf[fresh * r : fresh * r + fresh, :] = tok[r].astype(F32)
    for i in range(rows // 16):
        v = xf[16 * i : 16 * i + 16, :]
        ms = jnp.mean(v * v, axis=-1, keepdims=True)
        nrm[16 * i : 16 * i + 16, :] = (v * lax.rsqrt(ms + EPSILON) * gain1[...].astype(F32).reshape(1, width)).astype(BF16)
    qf[...] = jnp.zeros_like(qf)
    kf[...] = jnp.zeros_like(kf)
    vf[...] = jnp.zeros_like(vf)

    row = lane_mask((rows, head), 0)
    position = lax.rem(row, fresh)
    for r in range(req_dev):
        position = position + jnp.where(row // fresh == r, lengths[s * req_dev + r], 0)
    angle = position.astype(F32) * freq[...]
    cos[...] = jnp.cos(angle)
    sin[...] = jnp.where(lane_mask((rows, head), 1) < head // 2, -1.0, 1.0) * jnp.sin(angle)

    def rope(v):
        return v * cos[...] + pltpu.roll(v, head // 2, 1) * sin[...]

    heads = kv * group
    loads[0].wait()
    loads[3].start()
    loads[4].start()
    for lo in range(0, heads * head, 256):
        hi = min(lo + 256, heads * head)
        prod = mm(nrm[...], wq_v[:, lo:hi])
        for h in range(lo // head, hi // head):
            qkv[h] = rope(prod[:, h * head - lo : (h + 1) * head - lo])
    loads[1].wait()
    prod = mm(nrm[...], wk_v[...])
    for h in range(kv):
        qkv[heads + h] = rope(prod[:, h * head : (h + 1) * head])
    loads[2].wait()
    prod = mm(nrm[...], wv_v[...])
    for h in range(kv):
        qkv[heads + kv + h] = prod[:, h * head : (h + 1) * head]
    for n in range(fresh):
        src = pl.ds(n, req_dev, stride=fresh)
        for h in range(kv):
            for g in range(group):
                qf[h, pl.ds(g * fresh + n, req_dev, stride=ROWS), :] = qkv[h * group + g, src, :]
            kf[h, pl.ds(n, req_dev, stride=ROWS), :] = qkv[heads + h, src, :]
            vf[h, pl.ds(n, req_dev, stride=ROWS), :] = qkv[heads + kv + h, src, :]
    for h in range(kv):
        qs[h] = qf[h].astype(BF16)
        ks[h] = kf[h].astype(BF16)
        vs[h] = vf[h].astype(BF16)

    pl.semaphore_wait(barrier, seqs + xs - 1)
    is_home = lax.rem(s, step) == 0
    home = s // step

    def query_copy(d):
        return pltpu.make_async_remote_copy(
            src_ref=ql.at[home], dst_ref=ql.at[home], send_sem=qsend.at[d - 1], recv_sem=qrecv.at[home],
            device_id=(lax.rem(s + d, seqs), t), device_id_type=MESH,
        )

    @pl.when(is_home)
    def _():
        ql[home] = qs[:, :ROWS, :]
        for d in range(1, seqs):
            query_copy(d).start()

    loads[5].start()
    loads[6].start()
    loads[3].wait()
    loads[4].wait()

    def entry(p):
        known = places[p] - 1
        slot = jnp.maximum(known, 0)
        request = page_request[slot]
        used = jnp.where(known < 0, 0, lengths[request] - page_block[slot] * page)
        return slot, used, request // STRIDE

    def short_step(i, carry):
        lane = lane_mask((ROWS, page), 1)
        token = lax.rem(lane_mask((ROWS, ROWS), 0), fresh)
        key = lane_mask((ROWS, ROWS), 1)
        for u in range(SHORT_UNROLL):
            r = i * SHORT_UNROLL + u
            span = pl.ds(pl.multiple_of(r * ROWS, ROWS), ROWS)
            entries = [entry(r * SHORT_BLK + b) for b in range(SHORT_BLK)]
            weights = []
            for h in range(kv):
                q = qs[h, span, :]
                keys = jnp.concatenate([kc_v[slot, h] for slot, _, _ in entries], axis=0)
                value = mm_t(q, keys) * scale
                tiles = [
                    jnp.where(lane < used, value[:, b * page : (b + 1) * page], NEGATIVE)
                    for b, (_, used, _) in enumerate(entries)
                ]
                fresh_s = jnp.where(key <= token, mm_t(q, ks[h, span, :]) * scale, NEGATIVE)
                top = functools.reduce(jnp.maximum, tiles)
                m = jnp.maximum(jnp.max(top, axis=1, keepdims=True), jnp.max(fresh_s, axis=1, keepdims=True))
                w_f = jnp.exp(fresh_s - m).astype(BF16)
                w = [jnp.exp(tile - m).astype(BF16) for tile in tiles]
                l = jnp.sum(w_f.astype(F32), axis=1, keepdims=True)
                l = l + jnp.sum(sum(part.astype(F32) for part in w), axis=1, keepdims=True)
                so[h, span, :] = mm(w_f, vs[h, span, :])
                sm[h, span, :] = jnp.broadcast_to(m, (ROWS, head))
                sl[h, span, :] = jnp.broadcast_to(l, (ROWS, head))
                weights.append(jnp.concatenate(w, axis=1))
            values = jnp.concatenate(
                [jnp.concatenate([vc_v[slot, h] for h in range(kv)], axis=1) for slot, _, _ in entries], axis=0
            )
            o = mm(jnp.concatenate(weights, axis=0), values)
            for h in range(kv):
                so[h, span, :] += o[h * ROWS : (h + 1) * ROWS, h * head : (h + 1) * head]
        return carry

    loads[7].start()
    loads[8].start()
    lax.fori_loop(0, SHORT_FIRST, short_step, 0)

    for j in range(n_long):
        @pl.when(s != j * step)
        def _():
            pltpu.make_async_remote_copy(
                src_ref=ql.at[j], dst_ref=ql.at[j], send_sem=qsend.at[0], recv_sem=qrecv.at[j],
                device_id=mate, device_id_type=MESH,
            ).wait_recv()

    first = req_dev * SHORT_BLK

    def long_step(i, carry):
        lane = lane_mask((ROWS, page), 1)
        entries = [entry(first + i * UNROLL + u) for u in range(UNROLL)]
        places_of = [(u, h) for u in range(UNROLL) for h in range(kv)]
        pairs_of = [places_of[n : n + 2] for n in range(0, len(places_of), 2)]
        scores = []
        for pair in pairs_of:
            q = jnp.concatenate([ql[entries[u][2], h] for u, h in pair], axis=0)
            keys = jnp.concatenate([kc_v[entries[u][0], h] for u, h in pair], axis=0)
            value = mm_t(q, keys) * scale
            for n, (u, _) in enumerate(pair):
                part = value[n * ROWS : (n + 1) * ROWS, n * page : (n + 1) * page]
                scores.append(jnp.where(lane < entries[u][1], part, NEGATIVE))
        tops = [jnp.max(v, axis=1, keepdims=True) for v in scores]
        for k, pair in enumerate(pairs_of):
            weights = []
            for n, (u, h) in enumerate(pair):
                v, m = scores[2 * k + n], tops[2 * k + n]
                w = jnp.where(lane < entries[u][1], jnp.exp(v - m), 0.0).astype(BF16)
                om[i * UNROLL + u, h] = jnp.broadcast_to(m, (ROWS, head))
                ol[i * UNROLL + u, h] = jnp.broadcast_to(jnp.sum(w.astype(F32), axis=1, keepdims=True), (ROWS, head))
                weights.append(w)
            values = jnp.concatenate([vc_v[entries[u][0], h] for u, h in pair], axis=1)
            o = mm(jnp.concatenate(weights, axis=0), values)
            for n, (u, h) in enumerate(pair):
                oo[i * UNROLL + u, h] = o[n * ROWS : (n + 1) * ROWS, n * head : (n + 1) * head]
        return carry

    lax.fori_loop(0, others // UNROLL, long_step, 0)

    def top_step(i, carry):
        for u in range(4):
            p = i * 4 + u
            m = om[p]
            owner = entry(first + p)[2]
            carry = tuple(jnp.maximum(carry[j], m + jnp.where(owner == j, 0.0, NEGATIVE)) for j in range(n_long))
        return carry

    floor = jnp.full((kv, ROWS, head), FLOOR, F32)
    tops = lax.fori_loop(0, others // 4, top_step, (floor,) * n_long)
    for j in range(n_long):
        mj[j] = tops[j]

    def sum_step(i, carry):
        sums, totals = carry
        for u in range(4):
            p = i * 4 + u
            owner = entry(first + p)[2]
            e = jnp.exp(om[p] - mj[owner])
            o = e * oo[p]
            l = e * ol[p]
            marks = [jnp.where(owner == j, 1.0, 0.0) for j in range(n_long)]
            sums = tuple(sums[j] + marks[j] * o for j in range(n_long))
            totals = tuple(totals[j] + marks[j] * l for j in range(n_long))
        return sums, totals

    zero = jnp.zeros((kv, ROWS, head), F32)
    sums, totals = lax.fori_loop(0, others // 4, sum_step, ((zero,) * n_long, (zero,) * n_long))
    low = lane_mask((ROWS, head), 1) < head // 2
    for j in range(n_long):
        for h in range(kv):
            pj[j, h, 0] = sums[j][h]
            pj[j, h, 1] = jnp.where(low, tops[j][h], totals[j][h])

    def part_copy(j):
        return pltpu.make_async_remote_copy(
            src_ref=pj.at[j], dst_ref=parts.at[s], send_sem=psend.at[j], recv_sem=precv.at[s],
            device_id=(j * step, t), device_id_type=MESH,
        )

    for j in range(n_long):
        @pl.when(s != j * step)
        def _():
            part_copy(j).start()

    lax.fori_loop(SHORT_FIRST, req_dev // SHORT_UNROLL, short_step, 0)

    @pl.when(is_home)
    def _():
        for d in range(1, seqs):
            src = lax.rem(s + d, seqs)
            pltpu.make_async_remote_copy(
                src_ref=pj.at[0], dst_ref=parts.at[src], send_sem=psend.at[0], recv_sem=precv.at[src],
                device_id=mate, device_id_type=MESH,
            ).wait_recv()
        for h in range(kv):
            pieces = [(sm[h, :ROWS, :1], sl[h, :ROWS, :1], so[h, :ROWS, :])]
            blocks = [(pj[home, h, 0], pj[home, h, 1])]
            for d in range(1, seqs):
                src = lax.rem(s + d, seqs)
                blocks.append((parts[src, h, 0], parts[src, h, 1]))
            for o, ml in blocks:
                pieces.append((ml[:, :1], ml[:, head // 2 : head // 2 + 1], o))
            m = functools.reduce(jnp.maximum, [piece[0] for piece in pieces])
            l = jnp.zeros((ROWS, 1), F32)
            o = jnp.zeros((ROWS, head), F32)
            for m_i, l_i, o_i in pieces:
                e = jnp.exp(m_i - m)
                l = l + e * l_i
                o = o + e * o_i
            so[h, :ROWS, :] = o
            sl[h, :ROWS, :] = jnp.broadcast_to(l, (ROWS, head))

    for n in range(fresh):
        for h in range(kv):
            for g in range(group):
                src = pl.ds(g * fresh + n, req_dev, stride=ROWS)
                qkv[h * group + g, pl.ds(n, req_dev, stride=fresh), :] = so[h, src, :] / sl[h, src, :]
    for h in range(heads):
        att[:, h * head : (h + 1) * head] = qkv[h].astype(BF16)

    def to_mate(src, dst, send, recv):
        return pltpu.make_async_remote_copy(
            src_ref=src, dst_ref=dst, send_sem=send, recv_sem=recv, device_id=mate, device_id_type=MESH
        )

    def across(src, dst, send, recv, d):
        return pltpu.make_async_remote_copy(
            src_ref=src, dst_ref=dst, send_sem=send, recv_sem=recv,
            device_id=(s, lax.rem(x + d, xs) * 2 + c), device_id_type=MESH,
        )

    def block(ref, b):
        return ref[:, pl.ds(pl.multiple_of(b * bw, 128), bw)]

    loads[5].wait()
    started = []
    first_sum = [to_mate(s1.at[k], r1.at[k], s1_sem.at[k], r1_sem.at[k]) for k in range(xs)]
    crossing = {}
    for k in range(xs):
        s1[k] = mm(att[...], block(wo_v, (1 - c) * xs + k)).astype(BF16)
        first_sum[k].start()
        own[k] = mm(att[...], block(wo_v, c * xs + k))
        first_sum[k].wait_recv()
        total = own[k] + r1[k].astype(F32)
        own[k] = total
        s2[k] = total.astype(BF16)
        for d in range(1, xs):
            crossing[k, d] = across(s2.at[k], r2.at[d - 1, k], s2_sem.at[d - 1, k], r2_sem.at[d - 1, k], d)
            crossing[k, d].start()
    loads[6].wait()
    loads[7].wait()
    scales[...] = gain2[...].astype(F32).reshape(1, width)

    def feed(b, square):
        v = res[b].astype(F32)
        entering = (v * block(scales, b)).astype(BF16)
        span = pl.ds(pl.multiple_of(b * bw, 128), bw)
        for lo in range(0, act.shape[1], 256):
            gate = mm(entering, wg_v[span, lo : lo + 256])
            up = mm(entering, wu_v[span, lo : lo + 256])
            if square is None:
                gates[:, lo : lo + 256] = gate
                ups[:, lo : lo + 256] = up
            else:
                gates[:, lo : lo + 256] += gate
                ups[:, lo : lo + 256] += up
        more = jnp.sum(v * v, axis=-1, keepdims=True)
        return more if square is None else square + more

    square = None
    spread = []
    for k in range(xs):
        b = c * xs + k
        total = block(xf, b) + own[k]
        for d in range(1, xs):
            crossing[k, d].wait_recv()
            total = total + r2[d - 1, k].astype(F32)
        res[b] = total.astype(BF16)
        copy = to_mate(res.at[b], res.at[b], s3_sem.at[k], r3_sem.at[k])
        copy.start()
        spread.append(copy)
        square = feed(b, square)
    for k in range(xs):
        b = (1 - c) * xs + k
        to_mate(res.at[b], res.at[b], s3_sem.at[k], r3_sem.at[k]).wait_recv()
        square = feed(b, square)
    inverse = lax.rsqrt(square / width + EPSILON)
    for lo in range(0, act.shape[1], 256):
        gate = gates[:, lo : lo + 256] * inverse
        up = ups[:, lo : lo + 256] * inverse
        act[:, lo : lo + 256] = (gate / (1.0 + jnp.exp(-gate)) * up).astype(BF16)

    loads[8].wait()
    pair_sum, last = [], []
    for k in range(xs):
        to = lax.rem(x + 1 + k, xs)
        s4[k] = mm(act[...], block(wd_v, to * 2 + 1 - c)).astype(BF16)
        copy = to_mate(s4.at[k], r4.at[k], s4_sem.at[k], r4_sem.at[k])
        copy.start()
        pair_sum.append(copy)
        total = mm(act[...], block(wd_v, to * 2 + c))
        pair_sum[k].wait_recv()
        total = total + r4[k].astype(F32)
        if k < xs - 1:
            s5[k] = total.astype(BF16)
            copy = across(s5.at[k], r5.at[k], s5_sem.at[k], r5_sem.at[k], k + 1)
            copy.start()
            last.append(copy)
        else:
            total = total + res[t].astype(F32)
            for copy, d in zip(last, range(xs)):
                copy.wait_recv()
                total = total + r5[d].astype(F32)
            for r in range(req_dev):
                out[r] = total[fresh * r : fresh * r + fresh].astype(BF16)

    @pl.when(is_home)
    def _():
        for d in range(1, seqs):
            query_copy(d).wait_send()

    for j in range(n_long):
        @pl.when(s != j * step)
        def _():
            part_copy(j).wait_send()

    for copy in first_sum + list(crossing.values()) + spread + pair_sum + last:
        copy.wait_send()


def per_device(
    tokens, lengths, page_request, page_block, k_cache, v_cache, attn_gain, w_query, w_key, w_value,
    w_out, mlp_gain, w_gate, w_up, w_down,
):
    req_dev, fresh, width = tokens.shape
    slots, kv, page, head = k_cache.shape
    group = w_query.shape[1] // (kv * head)
    rows = req_dev * fresh
    seqs, tens = lax.axis_size("seq"), lax.axis_size("tensor")
    xs = tens // 2
    bw = width // tens
    n_long = lengths.shape[0] // STRIDE
    hidden = w_gate.shape[1]
    home_row = lax.axis_index("seq") * req_dev

    inverse = ROPE_BASE ** (-np.arange(head // 2) * 2.0 / head)
    freq = np.concatenate([inverse, inverse])[None, :].astype(np.float32)

    first = req_dev * SHORT_BLK
    most = slots - first + SHORT_BLK * -(-req_dev // STRIDE)
    others = -(-most // UNROLL) * UNROLL

    is_short = (page_request % STRIDE != 0) & (page_block < SHORT_BLK)
    code = jnp.where(is_short, (page_request - home_row) * SHORT_BLK + page_block + 1, 0)
    line = lax.broadcasted_iota(jnp.int32, (slots, slots), 0)
    index = lax.broadcasted_iota(jnp.int32, (slots, slots), 1)
    rank = jnp.sum(jnp.where(jnp.maximum(code[None, :], index - line + 1) <= 0, 1, 0), axis=1)
    line = lax.broadcasted_iota(jnp.int32, (first + others, slots), 0)
    index = lax.broadcasted_iota(jnp.int32, (first + others, slots), 1)
    is_place = (code[None, :] - (line + 1) == 0) | (
        jnp.maximum(jnp.abs(rank[None, :] + (first - line)), code[None, :]) == 0
    )
    places = jnp.sum(jnp.where(is_place, index + 1, 0), axis=1)

    vm = lambda shape, dtype=F32: pltpu.VMEM(shape, dtype)
    dma = lambda *shape: pltpu.SemaphoreType.DMA(shape)
    whole = pl.BlockSpec(memory_space=pltpu.VMEM)
    stay = pl.BlockSpec(memory_space=pl.ANY)
    big = (w_query, w_key, w_value, w_out, w_gate, w_up, w_down, k_cache, v_cache)
    tall = (kv, req_dev * ROWS, head)
    scratch = [vm(a.shape, BF16) for a in big]
    scratch += [
        vm((rows, width)), vm((rows, head)), vm((rows, head)), vm((rows, width), BF16), vm((kv * (group + 2), rows, head)), vm(tall), vm(tall), vm(tall),
        vm(tall, BF16), vm(tall, BF16), vm(tall, BF16), vm(tall), vm(tall), vm(tall),
        vm((n_long, kv, ROWS, head), BF16),
        vm((others, kv, ROWS, head)), vm((others, kv, ROWS, head)), vm((others, kv, ROWS, head)),
        vm((n_long, kv, ROWS, head)), vm((n_long, kv, 2, ROWS, head)), vm((seqs, kv, 2, ROWS, head)),
        vm((rows, kv * group * head), BF16),
        vm((xs, rows, bw), BF16), vm((xs, rows, bw), BF16), vm((xs, rows, bw)),
        vm((xs, rows, bw), BF16), vm((xs - 1, xs, rows, bw), BF16), vm((tens, rows, bw), BF16),
        vm((1, width)), vm((rows, hidden)), vm((rows, hidden)), vm((rows, hidden), BF16),
        vm((xs, rows, bw), BF16), vm((xs, rows, bw), BF16), vm((xs - 1, rows, bw), BF16), vm((xs - 1, rows, bw), BF16),
        dma(9), dma(seqs - 1), dma(n_long), dma(n_long), dma(seqs),
        dma(xs), dma(xs), dma(xs - 1, xs), dma(xs - 1, xs), dma(xs), dma(xs), dma(xs), dma(xs), dma(xs - 1), dma(xs - 1),
    ]
    moved = sum(a.size for a in big) * 2
    out = pl.pallas_call(
        functools.partial(layer_kernel, seqs, tens, n_long, others, req_dev, fresh, group, kv),
        out_shape=jax.ShapeDtypeStruct((req_dev, fresh, bw), BF16),
        in_specs=[pl.BlockSpec(memory_space=pltpu.SMEM)] * 4 + [whole] * 4 + [stay] * 9,
        out_specs=whole,
        scratch_shapes=scratch,
        compiler_params=pltpu.CompilerParams(
            collective_id=0, has_side_effects=True, vmem_limit_bytes=60 * 1024 * 1024
        ),
        cost_estimate=pl.CostEstimate(flops=2 * rows * moved, bytes_accessed=moved, transcendentals=0),
        name="layer",
    )(
        places, lengths, page_request, page_block, tokens, attn_gain, mlp_gain, freq, *big,
    )
    return out


def solution(mesh):
    placed = (
        P("seq", None, None),
        P(),
        P("seq"),
        P("seq"),
        P("seq", "tensor", None, None),
        P("seq", "tensor", None, None),
        P(),
        P(None, "tensor"),
        P(None, "tensor"),
        P(None, "tensor"),
        P("tensor", None),
        P(),
        P(None, "tensor"),
        P(None, "tensor"),
        P("tensor", None),
    )
    return jax.shard_map(
        per_device, mesh=mesh, in_specs=placed, out_specs=P("seq", None, "tensor"), check_vma=False
    )
```

```python
import functools
import math

import jax
import jax.numpy as jnp
import numpy as np
from jax import lax
from jax.experimental import pallas as pl
from jax.experimental.pallas import tpu as pltpu
from jax.sharding import PartitionSpec as P

EPSILON = 1e-05
NEGATIVE = -1e30
FLOOR = -1e20
ROPE_BASE = 500000.0
STRIDE = 32
SHORT_BLK = 4
ROWS = 16
UNROLL = 24
MERGE_UNROLL = 12
SHORT_UNROLL = 8
SHORT_FIRST = 1
MESH = pl.DeviceIdType.MESH
F32 = jnp.float32
BF16 = jnp.bfloat16


def mm(a, b):
    return jnp.dot(a, b, preferred_element_type=F32)


def mm_t(a, b):
    return lax.dot_general(a, b, (((1,), (1,)), ((), ())), preferred_element_type=F32)


def layer_kernel(
    seqs, tens, n_long, others, req_dev, fresh, group, kv,
    places, lengths, page_request, page_block, tok, gain1, gain2, freq, wq, wk, wv, wo, wg, wu, wd, kc, vc,
    out,
    wq_v, wk_v, wv_v, wo_v, wg_v, wu_v, wd_v, kc_v, vc_v,
    xf, cos, sin, nrm, qkv, qf, kf, vf, qs, ks, vs, so, sm, sl, ql, oo, om, ol, mj, pj, parts,
    att, s1, r1, own, s2, r2, res, scales, gates, ups, act, s4, r4, s5, r5,
    w_sem, qsend, qrecv, psend, precv,
    s1_sem, r1_sem, s2_sem, r2_sem, s3_sem, r3_sem, s4_sem, r4_sem, s5_sem, r5_sem,
):
    s = lax.axis_index("seq")
    t = lax.axis_index("tensor")
    c = lax.rem(t, 2)
    x = t // 2
    xs = tens // 2
    step = STRIDE // req_dev
    rows, width = xf.shape
    bw = width // tens
    head = kc.shape[-1]
    page = kc.shape[2]
    scale = 1.0 / math.sqrt(head)
    mate = (s, t + 1 - 2 * c)
    lane_mask = functools.partial(lax.broadcasted_iota, jnp.int32)

    pairs = ((wq, wq_v), (wk, wk_v), (wv, wv_v), (kc, kc_v), (vc, vc_v), (wo, wo_v), (wg, wg_v), (wu, wu_v), (wd, wd_v))
    loads = [pltpu.make_async_copy(a, b, w_sem.at[i]) for i, (a, b) in enumerate(pairs)]
    for i in range(3):
        loads[i].start()

    barrier = pltpu.get_barrier_semaphore()
    for d in range(1, seqs):
        pl.semaphore_signal(barrier, inc=1, device_id=(lax.rem(s + d, seqs), t), device_id_type=MESH)
    pl.semaphore_signal(barrier, inc=1, device_id=mate, device_id_type=MESH)
    for d in range(1, xs):
        pl.semaphore_signal(barrier, inc=1, device_id=(s, lax.rem(x + d, xs) * 2 + c), device_id_type=MESH)

    for r in range(req_dev):
        xf[fresh * r : fresh * r + fresh, :] = tok[r].astype(F32)
    for i in range(rows // 16):
        v = xf[16 * i : 16 * i + 16, :]
        ms = jnp.mean(v * v, axis=-1, keepdims=True)
        nrm[16 * i : 16 * i + 16, :] = (v * lax.rsqrt(ms + EPSILON) * gain1[...].astype(F32).reshape(1, width)).astype(BF16)
    qf[...] = jnp.zeros_like(qf)
    kf[...] = jnp.zeros_like(kf)
    vf[...] = jnp.zeros_like(vf)

    row = lane_mask((rows, head), 0)
    position = lax.rem(row, fresh)
    for r in range(req_dev):
        position = position + jnp.where(row // fresh == r, lengths[s * req_dev + r], 0)
    angle = position.astype(F32) * freq[...]
    cos[...] = jnp.cos(angle)
    sin[...] = jnp.where(lane_mask((rows, head), 1) < head // 2, -1.0, 1.0) * jnp.sin(angle)

    def rope(v):
        return v * cos[...] + pltpu.roll(v, head // 2, 1) * sin[...]

    heads = kv * group
    loads[0].wait()
    loads[3].start()
    loads[4].start()
    for lo in range(0, heads * head, 256):
        hi = min(lo + 256, heads * head)
        prod = mm(nrm[...], wq_v[:, lo:hi])
        for h in range(lo // head, hi // head):
            qkv[h] = rope(prod[:, h * head - lo : (h + 1) * head - lo])
    loads[1].wait()
    prod = mm(nrm[...], wk_v[...])
    for h in range(kv):
        qkv[heads + h] = rope(prod[:, h * head : (h + 1) * head])
    loads[2].wait()
    prod = mm(nrm[...], wv_v[...])
    for h in range(kv):
        qkv[heads + kv + h] = prod[:, h * head : (h + 1) * head]
    for n in range(fresh):
        src = pl.ds(n, req_dev, stride=fresh)
        for h in range(kv):
            for g in range(group):
                qf[h, pl.ds(g * fresh + n, req_dev, stride=ROWS), :] = qkv[h * group + g, src, :]
            kf[h, pl.ds(n, req_dev, stride=ROWS), :] = qkv[heads + h, src, :]
            vf[h, pl.ds(n, req_dev, stride=ROWS), :] = qkv[heads + kv + h, src, :]
    for h in range(kv):
        qs[h] = qf[h].astype(BF16)
        ks[h] = kf[h].astype(BF16)
        vs[h] = vf[h].astype(BF16)

    pl.semaphore_wait(barrier, seqs + xs - 1)
    is_home = lax.rem(s, step) == 0
    home = s // step

    def query_copy(d):
        return pltpu.make_async_remote_copy(
            src_ref=ql.at[home], dst_ref=ql.at[home], send_sem=qsend.at[d - 1], recv_sem=qrecv.at[home],
            device_id=(lax.rem(s + d, seqs), t), device_id_type=MESH,
        )

    @pl.when(is_home)
    def _():
        ql[home] = qs[:, :ROWS, :]
        for d in range(1, seqs):
            query_copy(d).start()

    loads[5].start()
    loads[6].start()
    loads[3].wait()
    loads[4].wait()

    def entry(p):
        known = places[p] - 1
        slot = jnp.maximum(known, 0)
        request = page_request[slot]
        used = jnp.where(known < 0, 0, lengths[request] - page_block[slot] * page)
        return slot, used, request // STRIDE

    def short_step(i, carry):
        lane = lane_mask((ROWS, page), 1)
        token = lax.rem(lane_mask((ROWS, ROWS), 0), fresh)
        key = lane_mask((ROWS, ROWS), 1)
        for u in range(SHORT_UNROLL):
            r = i * SHORT_UNROLL + u
            span = pl.ds(pl.multiple_of(r * ROWS, ROWS), ROWS)
            entries = [entry(r * SHORT_BLK + b) for b in range(SHORT_BLK)]
            weights = []
            for h in range(kv):
                q = qs[h, span, :]
                keys = jnp.concatenate([kc_v[slot, h] for slot, _, _ in entries], axis=0)
                value = mm_t(q, keys) * scale
                tiles = [
                    jnp.where(lane < used, value[:, b * page : (b + 1) * page], NEGATIVE)
                    for b, (_, used, _) in enumerate(entries)
                ]
                fresh_s = jnp.where(key <= token, mm_t(q, ks[h, span, :]) * scale, NEGATIVE)
                top = functools.reduce(jnp.maximum, tiles)
                m = jnp.maximum(jnp.max(top, axis=1, keepdims=True), jnp.max(fresh_s, axis=1, keepdims=True))
                w_f = jnp.exp(fresh_s - m).astype(BF16)
                w = [jnp.exp(tile - m).astype(BF16) for tile in tiles]
                l = jnp.sum(w_f.astype(F32), axis=1, keepdims=True)
                l = l + jnp.sum(sum(part.astype(F32) for part in w), axis=1, keepdims=True)
                so[h, span, :] = mm(w_f, vs[h, span, :])
                sm[h, span, :] = jnp.broadcast_to(m, (ROWS, head))
                sl[h, span, :] = jnp.broadcast_to(l, (ROWS, head))
                weights.append(jnp.concatenate(w, axis=1))
            values = jnp.concatenate(
                [jnp.concatenate([vc_v[slot, h] for h in range(kv)], axis=1) for slot, _, _ in entries], axis=0
            )
            o = mm(jnp.concatenate(weights, axis=0), values)
            for h in range(kv):
                so[h, span, :] += o[h * ROWS : (h + 1) * ROWS, h * head : (h + 1) * head]
        return carry

    loads[7].start()
    loads[8].start()
    lax.fori_loop(0, SHORT_FIRST, short_step, 0)

    for j in range(n_long):
        @pl.when(s != j * step)
        def _():
            pltpu.make_async_remote_copy(
                src_ref=ql.at[j], dst_ref=ql.at[j], send_sem=qsend.at[0], recv_sem=qrecv.at[j],
                device_id=mate, device_id_type=MESH,
            ).wait_recv()

    first = req_dev * SHORT_BLK

    def long_step(i, carry):
        lane = lane_mask((ROWS, page), 1)
        entries = [entry(first + i * UNROLL + u) for u in range(UNROLL)]
        places_of = [(u, h) for u in range(UNROLL) for h in range(kv)]
        pairs_of = [places_of[n : n + 2] for n in range(0, len(places_of), 2)]
        scores = []
        for pair in pairs_of:
            q = jnp.concatenate([ql[entries[u][2], h] for u, h in pair], axis=0)
            keys = jnp.concatenate([kc_v[entries[u][0], h] for u, h in pair], axis=0)
            value = mm_t(q, keys) * scale
            for n, (u, _) in enumerate(pair):
                part = value[n * ROWS : (n + 1) * ROWS, n * page : (n + 1) * page]
                scores.append(jnp.where(lane < entries[u][1], part, NEGATIVE))
        tops = [jnp.max(v, axis=1, keepdims=True) for v in scores]
        for k, pair in enumerate(pairs_of):
            weights = []
            for n, (u, h) in enumerate(pair):
                v, m = scores[2 * k + n], tops[2 * k + n]
                w = jnp.where(lane < entries[u][1], jnp.exp(v - m), 0.0).astype(BF16)
                om[i * UNROLL + u, h] = jnp.broadcast_to(m, (ROWS, head))
                ol[i * UNROLL + u, h] = jnp.broadcast_to(jnp.sum(w.astype(F32), axis=1, keepdims=True), (ROWS, head))
                weights.append(w)
            values = jnp.concatenate([vc_v[entries[u][0], h] for u, h in pair], axis=1)
            o = mm(jnp.concatenate(weights, axis=0), values)
            for n, (u, h) in enumerate(pair):
                oo[i * UNROLL + u, h] = o[n * ROWS : (n + 1) * ROWS, n * head : (n + 1) * head]
        return carry

    lax.fori_loop(0, others // UNROLL, long_step, 0)

    def top_step(i, carry):
        for u in range(MERGE_UNROLL):
            p = i * MERGE_UNROLL + u
            m = om[p]
            owner = entry(first + p)[2]
            carry = tuple(jnp.maximum(carry[j], m + jnp.where(owner == j, 0.0, NEGATIVE)) for j in range(n_long))
        return carry

    floor = jnp.full((kv, ROWS, head), FLOOR, F32)
    tops = lax.fori_loop(0, others // MERGE_UNROLL, top_step, (floor,) * n_long)
    for j in range(n_long):
        mj[j] = tops[j]

    def sum_step(i, carry):
        sums, totals = carry
        for u in range(MERGE_UNROLL):
            p = i * MERGE_UNROLL + u
            owner = entry(first + p)[2]
            e = jnp.exp(om[p] - mj[owner])
            o = e * oo[p]
            l = e * ol[p]
            marks = [jnp.where(owner == j, 1.0, 0.0) for j in range(n_long)]
            sums = tuple(sums[j] + marks[j] * o for j in range(n_long))
            totals = tuple(totals[j] + marks[j] * l for j in range(n_long))
        return sums, totals

    zero = jnp.zeros((kv, ROWS, head), F32)
    sums, totals = lax.fori_loop(0, others // MERGE_UNROLL, sum_step, ((zero,) * n_long, (zero,) * n_long))
    lanes = head // (2 * kv)
    part_of = lane_mask((ROWS, head), 1) // lanes
    for j in range(n_long):
        for h in range(kv):
            pj[j, h] = sums[j][h]
        packed = tops[j][0]
        for h in range(kv):
            packed = jnp.where(part_of == 2 * h, tops[j][h], packed)
            packed = jnp.where(part_of == 2 * h + 1, totals[j][h], packed)
        pj[j, kv] = packed

    def part_copy(j):
        return pltpu.make_async_remote_copy(
            src_ref=pj.at[j], dst_ref=parts.at[s], send_sem=psend.at[j], recv_sem=precv.at[s],
            device_id=(j * step, t), device_id_type=MESH,
        )

    for j in range(n_long):
        @pl.when(s != j * step)
        def _():
            part_copy(j).start()

    lax.fori_loop(SHORT_FIRST, req_dev // SHORT_UNROLL, short_step, 0)

    @pl.when(is_home)
    def _():
        for d in range(1, seqs):
            src = lax.rem(s + d, seqs)
            pltpu.make_async_remote_copy(
                src_ref=pj.at[0], dst_ref=parts.at[src], send_sem=psend.at[0], recv_sem=precv.at[src],
                device_id=mate, device_id_type=MESH,
            ).wait_recv()
        for h in range(kv):
            pieces = [(sm[h, :ROWS, :1], sl[h, :ROWS, :1], so[h, :ROWS, :])]
            blocks = [(pj[home, h], pj[home, kv])]
            for d in range(1, seqs):
                src = lax.rem(s + d, seqs)
                blocks.append((parts[src, h], parts[src, kv]))
            for o, ml in blocks:
                pieces.append((ml[:, 2 * h * lanes : 2 * h * lanes + 1], ml[:, (2 * h + 1) * lanes : (2 * h + 1) * lanes + 1], o))
            m = functools.reduce(jnp.maximum, [piece[0] for piece in pieces])
            l = jnp.zeros((ROWS, 1), F32)
            o = jnp.zeros((ROWS, head), F32)
            for m_i, l_i, o_i in pieces:
                e = jnp.exp(m_i - m)
                l = l + e * l_i
                o = o + e * o_i
            so[h, :ROWS, :] = o
            sl[h, :ROWS, :] = jnp.broadcast_to(l, (ROWS, head))

    for n in range(fresh):
        for h in range(kv):
            for g in range(group):
                src = pl.ds(g * fresh + n, req_dev, stride=ROWS)
                qkv[h * group + g, pl.ds(n, req_dev, stride=fresh), :] = so[h, src, :] / sl[h, src, :]
    for h in range(heads):
        att[:, h * head : (h + 1) * head] = qkv[h].astype(BF16)

    def to_mate(src, dst, send, recv):
        return pltpu.make_async_remote_copy(
            src_ref=src, dst_ref=dst, send_sem=send, recv_sem=recv, device_id=mate, device_id_type=MESH
        )

    def across(src, dst, send, recv, d):
        return pltpu.make_async_remote_copy(
            src_ref=src, dst_ref=dst, send_sem=send, recv_sem=recv,
            device_id=(s, lax.rem(x + d, xs) * 2 + c), device_id_type=MESH,
        )

    def block(ref, b):
        return ref[:, pl.ds(pl.multiple_of(b * bw, 128), bw)]

    loads[5].wait()
    started = []
    first_sum = [to_mate(s1.at[k], r1.at[k], s1_sem.at[k], r1_sem.at[k]) for k in range(xs)]
    crossing = {}
    for k in range(xs):
        s1[k] = mm(att[...], block(wo_v, (1 - c) * xs + k)).astype(BF16)
        first_sum[k].start()
        own[k] = mm(att[...], block(wo_v, c * xs + k))
        first_sum[k].wait_recv()
        total = own[k] + r1[k].astype(F32)
        own[k] = total
        s2[k] = total.astype(BF16)
        for d in range(1, xs):
            crossing[k, d] = across(s2.at[k], r2.at[d - 1, k], s2_sem.at[d - 1, k], r2_sem.at[d - 1, k], d)
            crossing[k, d].start()
    loads[6].wait()
    loads[7].wait()
    scales[...] = gain2[...].astype(F32).reshape(1, width)

    def feed(b, square):
        v = res[b].astype(F32)
        entering = (v * block(scales, b)).astype(BF16)
        span = pl.ds(pl.multiple_of(b * bw, 128), bw)
        for lo in range(0, act.shape[1], 256):
            gate = mm(entering, wg_v[span, lo : lo + 256])
            up = mm(entering, wu_v[span, lo : lo + 256])
            if square is None:
                gates[:, lo : lo + 256] = gate
                ups[:, lo : lo + 256] = up
            else:
                gates[:, lo : lo + 256] += gate
                ups[:, lo : lo + 256] += up
        more = jnp.sum(v * v, axis=-1, keepdims=True)
        return more if square is None else square + more

    square = None
    spread = []
    for k in range(xs):
        b = c * xs + k
        total = block(xf, b) + own[k]
        for d in range(1, xs):
            crossing[k, d].wait_recv()
            total = total + r2[d - 1, k].astype(F32)
        res[b] = total.astype(BF16)
        copy = to_mate(res.at[b], res.at[b], s3_sem.at[k], r3_sem.at[k])
        copy.start()
        spread.append(copy)
        square = feed(b, square)
    for k in range(xs):
        b = (1 - c) * xs + k
        to_mate(res.at[b], res.at[b], s3_sem.at[k], r3_sem.at[k]).wait_recv()
        square = feed(b, square)
    inverse = lax.rsqrt(square / width + EPSILON)
    for lo in range(0, act.shape[1], 256):
        gate = gates[:, lo : lo + 256] * inverse
        up = ups[:, lo : lo + 256] * inverse
        act[:, lo : lo + 256] = (gate / (1.0 + jnp.exp(-gate)) * up).astype(BF16)

    loads[8].wait()
    pair_sum, last = [], []
    for k in range(xs):
        to = lax.rem(x + 1 + k, xs)
        s4[k] = mm(act[...], block(wd_v, to * 2 + 1 - c)).astype(BF16)
        copy = to_mate(s4.at[k], r4.at[k], s4_sem.at[k], r4_sem.at[k])
        copy.start()
        pair_sum.append(copy)
        total = mm(act[...], block(wd_v, to * 2 + c))
        pair_sum[k].wait_recv()
        total = total + r4[k].astype(F32)
        if k < xs - 1:
            s5[k] = total.astype(BF16)
            copy = across(s5.at[k], r5.at[k], s5_sem.at[k], r5_sem.at[k], k + 1)
            copy.start()
            last.append(copy)
        else:
            total = total + res[t].astype(F32)
            for copy, d in zip(last, range(xs)):
                copy.wait_recv()
                total = total + r5[d].astype(F32)
            for r in range(req_dev):
                out[r] = total[fresh * r : fresh * r + fresh].astype(BF16)

    @pl.when(is_home)
    def _():
        for d in range(1, seqs):
            query_copy(d).wait_send()

    for j in range(n_long):
        @pl.when(s != j * step)
        def _():
            part_copy(j).wait_send()

    for copy in first_sum + list(crossing.values()) + spread + pair_sum + last:
        copy.wait_send()


def per_device(
    tokens, lengths, page_request, page_block, k_cache, v_cache, attn_gain, w_query, w_key, w_value,
    w_out, mlp_gain, w_gate, w_up, w_down,
):
    req_dev, fresh, width = tokens.shape
    slots, kv, page, head = k_cache.shape
    group = w_query.shape[1] // (kv * head)
    rows = req_dev * fresh
    seqs, tens = lax.axis_size("seq"), lax.axis_size("tensor")
    xs = tens // 2
    bw = width // tens
    n_long = lengths.shape[0] // STRIDE
    hidden = w_gate.shape[1]
    home_row = lax.axis_index("seq") * req_dev

    inverse = ROPE_BASE ** (-np.arange(head // 2) * 2.0 / head)
    freq = np.concatenate([inverse, inverse])[None, :].astype(np.float32)

    first = req_dev * SHORT_BLK
    most = slots - first + SHORT_BLK * -(-req_dev // STRIDE)
    others = -(-most // UNROLL) * UNROLL

    is_short = (page_request % STRIDE != 0) & (page_block < SHORT_BLK)
    code = jnp.where(is_short, (page_request - home_row) * SHORT_BLK + page_block + 1, 0)
    line = lax.broadcasted_iota(jnp.int32, (slots, slots), 0)
    index = lax.broadcasted_iota(jnp.int32, (slots, slots), 1)
    rank = jnp.sum(jnp.where(jnp.maximum(code[None, :], index - line + 1) <= 0, 1, 0), axis=1)
    line = lax.broadcasted_iota(jnp.int32, (first + others, slots), 0)
    index = lax.broadcasted_iota(jnp.int32, (first + others, slots), 1)
    is_place = (code[None, :] - (line + 1) == 0) | (
        jnp.maximum(jnp.abs(rank[None, :] + (first - line)), code[None, :]) == 0
    )
    places = jnp.sum(jnp.where(is_place, index + 1, 0), axis=1)

    vm = lambda shape, dtype=F32: pltpu.VMEM(shape, dtype)
    dma = lambda *shape: pltpu.SemaphoreType.DMA(shape)
    whole = pl.BlockSpec(memory_space=pltpu.VMEM)
    stay = pl.BlockSpec(memory_space=pl.ANY)
    big = (w_query, w_key, w_value, w_out, w_gate, w_up, w_down, k_cache, v_cache)
    tall = (kv, req_dev * ROWS, head)
    scratch = [vm(a.shape, BF16) for a in big]
    scratch += [
        vm((rows, width)), vm((rows, head)), vm((rows, head)), vm((rows, width), BF16), vm((kv * (group + 2), rows, head)), vm(tall), vm(tall), vm(tall),
        vm(tall, BF16), vm(tall, BF16), vm(tall, BF16), vm(tall), vm(tall), vm(tall),
        vm((n_long, kv, ROWS, head), BF16),
        vm((others, kv, ROWS, head)), vm((others, kv, ROWS, head)), vm((others, kv, ROWS, head)),
        vm((n_long, kv, ROWS, head)), vm((n_long, kv + 1, ROWS, head)), vm((seqs, kv + 1, ROWS, head)),
        vm((rows, kv * group * head), BF16),
        vm((xs, rows, bw), BF16), vm((xs, rows, bw), BF16), vm((xs, rows, bw)),
        vm((xs, rows, bw), BF16), vm((xs - 1, xs, rows, bw), BF16), vm((tens, rows, bw), BF16),
        vm((1, width)), vm((rows, hidden)), vm((rows, hidden)), vm((rows, hidden), BF16),
        vm((xs, rows, bw), BF16), vm((xs, rows, bw), BF16), vm((xs - 1, rows, bw), BF16), vm((xs - 1, rows, bw), BF16),
        dma(9), dma(seqs - 1), dma(n_long), dma(n_long), dma(seqs),
        dma(xs), dma(xs), dma(xs - 1, xs), dma(xs - 1, xs), dma(xs), dma(xs), dma(xs), dma(xs), dma(xs - 1), dma(xs - 1),
    ]
    moved = sum(a.size for a in big) * 2
    out = pl.pallas_call(
        functools.partial(layer_kernel, seqs, tens, n_long, others, req_dev, fresh, group, kv),
        out_shape=jax.ShapeDtypeStruct((req_dev, fresh, bw), BF16),
        in_specs=[pl.BlockSpec(memory_space=pltpu.SMEM)] * 4 + [whole] * 4 + [stay] * 9,
        out_specs=whole,
        scratch_shapes=scratch,
        compiler_params=pltpu.CompilerParams(
            collective_id=0, has_side_effects=True, vmem_limit_bytes=60 * 1024 * 1024
        ),
        cost_estimate=pl.CostEstimate(flops=2 * rows * moved, bytes_accessed=moved, transcendentals=0),
        name="layer",
    )(
        places, lengths, page_request, page_block, tokens, attn_gain, mlp_gain, freq, *big,
    )
    return out


def solution(mesh):
    placed = (
        P("seq", None, None),
        P(),
        P("seq"),
        P("seq"),
        P("seq", "tensor", None, None),
        P("seq", "tensor", None, None),
        P(),
        P(None, "tensor"),
        P(None, "tensor"),
        P(None, "tensor"),
        P("tensor", None),
        P(),
        P(None, "tensor"),
        P(None, "tensor"),
        P("tensor", None),
    )
    return jax.shard_map(
        per_device, mesh=mesh, in_specs=placed, out_specs=P("seq", None, "tensor"), check_vma=False
    )
```
